32 devices in a mesh: grid: 8 (over z, x), help: 4 (over y, core).
Axes of the slice: x: 2, y: 2, z: 4, core: 2. Of those that a mesh axis runs over, the one named last changes fastest.
Arguments:
- corners: float32 [24, 65536], P(None, 'grid'), as said below
- solution: float32 [40, 65536], P(None, 'grid'), may hold values from -6 to 6
- loc_xyz: float32 [3, 262144], P(None, ('grid', 'help')), as said below
- loc_cell: int32 [262144], P(('grid', 'help')), may hold values from 0 to 8191, as said below
- loc_live: int32 [8, 4], P('grid', 'help'), may hold values from 1 to 8192, 16384 in all within a row
- rem_xyz: float32 [3, 1024], P(None, ('grid', 'help')), as said below
- rem_cell: int32 [1024], P(('grid', 'help')), may hold values from 0 to 8191, as said below
- rem_count: int32 [32, 8], P(('grid', 'help')), may hold values from 1 to 4
Outputs:
- loc_values: float32 [5, 262144], P(None, ('grid', 'help'))
- rem_values: float32 [5, 1024], P(None, ('grid', 'help'))
The draws below stay inside these ranges and needn't reach their ends.
Inputs may be any that keep to these rules, and one draw needn't show every extreme that they name: `corners`: each cell's corner k lies within a quarter of the cell's half edge of the corner with signs s_k of an axis-aligned cube. `loc_xyz`: each receptor is the image under its donor cell's trilinear map of a point in the cube of half edge 0.9. `rem_xyz`: each receptor is the image under its donor cell's trilinear map of a point in the cube of half edge 0.9. `loc_cell`: a cell of the owner's partition. `rem_cell`: a cell of the partition named by the slot. `loc_live`: live slots are those of lowest rank on each device; in each help group one device has 8192 live slots and the group has 16384 in all. `rem_count`: live slots of a partition come first.
All inputs are finite; a program needn't handle non-finite values.
Results may differ from the reference program's by a relative error of at most 0.0003.
Values sent between devices are 32-bit elements; how exact they have to be, the bound alone decides.
No kernel may reach another device: no remote copies, remote signals or barrier semaphores. Data moves between devices by JAX's collectives and lax.ppermute only.
A program may use at most 64 MiB of HBM per device.

```python
import math
import jax
import jax.numpy as jnp
import numpy as np
from jax import lax

CELL_PART = 8192
LOC_DEV = 8192
CAP = 4
PASSES = 3
CELLS = 65536
REM_TOTAL = 1024
N_GRID = 8
N_HELP = 4
DEVICES = 32


def corner_table(key):
    salted = jax.random.fold_in(key, 7001)
    perturb_key, size_key, center_key = jax.random.split(salted, 3)
    cell_total = CELL_PART * N_GRID
    perturb = jax.random.uniform(perturb_key, (3, 8, cell_total), jnp.float32, -0.25, 0.25)
    cell_size = jnp.exp(jax.random.uniform(size_key, (1, 1, cell_total), jnp.float32, math.log(0.5), math.log(2.0)))
    center = jax.random.uniform(center_key, (3, 1, cell_total), jnp.float32, -2.0, 2.0)
    corner_no = jnp.arange(8, dtype=jnp.int32)
    corner_signs = jnp.stack([2.0 * (corner_no >> dim_idx & 1).astype(jnp.float32) - 1.0 for dim_idx in range(3)], 0)
    return (center + cell_size * (corner_signs[:, :, None] + perturb)).reshape(24, cell_total)


def cell_ids(key, salt_tag, total):
    return jax.random.randint(jax.random.fold_in(key, salt_tag), (total,), 0, CELL_PART, dtype=jnp.int32)


def mapped_points(key, salt_tag, global_cell):
    total = global_cell.shape[0]
    xi_key = jax.random.fold_in(key, salt_tag)
    local_xi = jax.random.uniform(xi_key, (3, total), jnp.float32, -0.9, 0.9)
    corner_rows = corner_table(key)
    outputs = []
    for row_idx in range(3):
        total_value = jnp.zeros((total,), jnp.float32)
        for corner in range(8):
            weight = jnp.ones((total,), jnp.float32)
            for dim_idx in range(3):
                if corner >> dim_idx & 1:
                    weight = weight * (1.0 + local_xi[dim_idx]) * 0.5
                else:
                    weight = weight * (1.0 - local_xi[dim_idx]) * 0.5
            total_value = total_value + weight * corner_rows[8 * row_idx + corner][global_cell]
        outputs.append(total_value)
    return jnp.stack(outputs, 0)


def draw_corners(key, part):
    return corner_table(key)


def draw_loc_cell(key, part):
    return cell_ids(key, 7101, LOC_DEV * N_GRID * N_HELP)


def draw_loc_xyz(key, part):
    total = LOC_DEV * N_GRID * N_HELP
    slot_no = jnp.arange(total, dtype=jnp.int32)
    device = slot_no // LOC_DEV
    global_cell = device // N_HELP * CELL_PART + cell_ids(key, 7101, total)
    return mapped_points(key, 7102, global_cell)


def draw_rem_cell(key, part):
    return cell_ids(key, 7201, CAP * N_GRID * N_GRID * N_HELP)


def draw_rem_xyz(key, part):
    total = CAP * N_GRID * N_GRID * N_HELP
    slot_no = jnp.arange(total, dtype=jnp.int32)
    partition = slot_no % N_GRID
    global_cell = partition * CELL_PART + cell_ids(key, 7201, total)
    return mapped_points(key, 7202, global_cell)


def place_ends(drawn, key, least, top_value):
    longest = drawn.shape.index(max(drawn.shape))
    spots = []
    for shift in (0, 1):
        where = [jax.random.randint(jax.random.fold_in(key, axis), (), 0, length) for axis, length in enumerate(drawn.shape)]
        where[longest] = (where[longest] + shift) % drawn.shape[longest]
        spots.append(tuple(where))
    return drawn.at[spots[0]].set(least).at[spots[1]].set(top_value)


def block_levels(own_key, dims, pieces, smallest, top_value):
    def one(dim, blocks):
        heights = jax.random.uniform(jax.random.fold_in(jax.random.fold_in(own_key, 6), dim), (blocks,), jnp.float32, smallest / len(pieces), top_value / len(pieces))
        return jnp.repeat(jnp.exp(heights), dims[dim] // blocks).reshape((-1,) + (1,) * (len(dims) - dim - 1))

    gain = one(*pieces[0])
    for cut in pieces[1:]:
        gain = gain * one(*cut)
    return gain


def profile(count, total, most, lean):
    portions = [(1 << 20) // math.isqrt(grade ** lean) + 1 for grade in range(2, count + 1)]
    spare, counts = total - most - (count - 1), [1] * (count - 1)
    while spare > 0:
        free = [i for i in range(count - 1) if counts[i] < most]
        whole, budget = sum([portions[i] for i in free]), spare
        for i in free:
            extra = min(most - counts[i], max(1, budget * portions[i] // whole), spare)
            counts[i] = counts[i] + extra
            spare = spare - extra
    return np.array([most] + counts)


def ragged_sizes(own_key, amount, total, reach, slope):
    if amount == 2:
        one = jax.random.randint(own_key, (), max(1, total - reach), min(reach, total - 1) + 1)
        return jnp.stack([one, total - one])
    tallies = jnp.asarray(profile(amount, total, reach, slope), jnp.int32)
    twos = (amount - 1) // 2
    source_of, sink = tallies[1:1 + 2 * twos:2], tallies[2:2 + 2 * twos:2]
    room = jnp.minimum(source_of - 1, reach - sink)
    shifted = jax.random.randint(jax.random.fold_in(own_key, 1), (twos,), 0, 1 << 20) % (room + 1)
    tallies = tallies.at[1:1 + 2 * twos:2].set(source_of - shifted).at[2:2 + 2 * twos:2].set(sink + shifted)
    return tallies[jax.random.permutation(jax.random.fold_in(own_key, 2), amount)]


def normal_values(key, dims, spread, reach, cuts=(), kind=jnp.bfloat16):
    entries = jax.random.normal(key, dims, jnp.float32) * spread
    if len(cuts) > 0:
        entries = block_levels(key, dims, cuts, -0.22, 0.18) * entries
    return jnp.clip(entries, min=-reach, max=reach).astype(kind)


def setup_inputs(seed: int = 0) -> dict:
    keys = jax.random.split(jax.random.key(seed), 9)
    corners = draw_corners(jax.random.fold_in(keys[8], 71), 0)
    solution = normal_values(keys[1], (40, CELLS), 1.0, 6.0, ((1, 8),), jnp.float32)
    loc_xyz = draw_loc_xyz(jax.random.fold_in(keys[8], 71), 0)
    loc_cell = draw_loc_cell(jax.random.fold_in(keys[8], 71), 0)
    loc_live = jax.vmap(lambda own: ragged_sizes(own, N_HELP, 2 * LOC_DEV, LOC_DEV, 2))(jax.random.split(keys[4], N_GRID)).reshape((N_GRID, N_HELP)).astype(jnp.int32)
    rem_xyz = draw_rem_xyz(jax.random.fold_in(keys[8], 71), 0)
    rem_cell = draw_rem_cell(jax.random.fold_in(keys[8], 71), 0)
    rem_count = place_ends(jax.random.randint(keys[7], (DEVICES, N_GRID), 1, CAP + 1), jax.random.fold_in(keys[7], 1), 1, CAP).astype(jnp.int32)
    return dict(corners=corners, solution=solution, loc_xyz=loc_xyz, loc_cell=loc_cell, loc_live=loc_live, rem_xyz=rem_xyz, rem_cell=rem_cell, rem_count=rem_count)


def solve_three(jacobian, residual):
    row_zero, row_one, row_two = jacobian
    cof_00 = row_one[1] * row_two[2] - row_one[2] * row_two[1]
    cof_01 = row_one[2] * row_two[0] - row_one[0] * row_two[2]
    cof_02 = row_one[0] * row_two[1] - row_one[1] * row_two[0]
    cof_10 = row_zero[2] * row_two[1] - row_zero[1] * row_two[2]
    cof_11 = row_zero[0] * row_two[2] - row_zero[2] * row_two[0]
    cof_12 = row_zero[1] * row_two[0] - row_zero[0] * row_two[1]
    cof_20 = row_zero[1] * row_one[2] - row_zero[2] * row_one[1]
    cof_21 = row_zero[2] * row_one[0] - row_zero[0] * row_one[2]
    cof_22 = row_zero[0] * row_one[1] - row_zero[1] * row_one[0]
    determinant = row_zero[0] * cof_00 + row_zero[1] * cof_01 + row_zero[2] * cof_02
    step_x = (cof_00 * residual[0] + cof_10 * residual[1] + cof_20 * residual[2]) / determinant
    step_y = (cof_01 * residual[0] + cof_11 * residual[1] + cof_21 * residual[2]) / determinant
    step_z = (cof_02 * residual[0] + cof_12 * residual[1] + cof_22 * residual[2]) / determinant
    return [step_x, step_y, step_z]


def corner_weights(local_xi):
    lower_half = [(1.0 - value) * 0.5 for value in local_xi]
    upper_half = [(1.0 + value) * 0.5 for value in local_xi]
    factors_all = []
    slopes_all = []
    for corner in range(8):
        factors = [upper_half[dim_idx] if (corner >> dim_idx) & 1 else lower_half[dim_idx] for dim_idx in range(3)]
        slopes = [0.5 if (corner >> dim_idx) & 1 else -0.5 for dim_idx in range(3)]
        factors_all.append(factors)
        slopes_all.append(slopes)
    return factors_all, slopes_all


def interpolate(points, blocks, fields):
    local_xi = [jnp.zeros_like(points[0]) for dim_idx in range(3)]
    for newton_pass in range(PASSES):
        factors_all, slopes_all = corner_weights(local_xi)
        residual = [-points[dim_idx] for dim_idx in range(3)]
        jacobian = [[jnp.zeros_like(points[0]) for col_idx in range(3)] for row_idx in range(3)]
        for corner in range(8):
            factors = factors_all[corner]
            slopes = slopes_all[corner]
            weight = factors[0] * factors[1] * factors[2]
            partials = [slopes[0] * factors[1] * factors[2], factors[0] * slopes[1] * factors[2], factors[0] * factors[1] * slopes[2]]
            for row_idx in range(3):
                corner_coord = blocks[8 * row_idx + corner]
                residual[row_idx] = residual[row_idx] + weight * corner_coord
                for col_idx in range(3):
                    jacobian[row_idx][col_idx] = jacobian[row_idx][col_idx] + partials[col_idx] * corner_coord
        newton_step = solve_three(jacobian, residual)
        local_xi = [local_xi[dim_idx] - newton_step[dim_idx] for dim_idx in range(3)]
    factors_all, slopes_all = corner_weights(local_xi)
    outputs = []
    for field_idx in range(5):
        total_value = jnp.zeros_like(points[0])
        for corner in range(8):
            factors = factors_all[corner]
            weight = factors[0] * factors[1] * factors[2]
            total_value = total_value + weight * fields[8 * field_idx + corner]
        outputs.append(total_value)
    return jnp.stack(outputs, 0)


def reference(corners, solution, loc_xyz, loc_cell, loc_live, rem_xyz, rem_cell, rem_count):
    device_total = N_GRID * N_HELP
    live_flat = loc_live.reshape(-1)
    slab = LOC_DEV // N_HELP
    slot_idx = jnp.arange(LOC_DEV, dtype=jnp.int32)
    slot_rank = (slot_idx % slab) * N_HELP + slot_idx // slab

    def local_block(inputs):
        point_block, cell_block, device = inputs
        cell_base = (device // N_HELP) * CELL_PART
        global_cell = (cell_block + cell_base).astype(jnp.int32)
        results = interpolate(point_block, jnp.take(corners, global_cell, axis=1), jnp.take(solution, global_cell, axis=1))
        live_count = live_flat[device]
        is_live = slot_rank < live_count
        return jnp.where(is_live[None, :], results, 0.0)

    point_blocks = loc_xyz.reshape(3, device_total, LOC_DEV).transpose(1, 0, 2)
    cell_blocks = loc_cell.reshape(device_total, LOC_DEV)
    device_ids = jnp.arange(device_total, dtype=jnp.int32)
    local_out = lax.map(local_block, (point_blocks, cell_blocks, device_ids))
    loc_values = local_out.transpose(1, 0, 2).reshape(5, device_total * LOC_DEV)

    slot_no = jnp.arange(REM_TOTAL, dtype=jnp.int32)
    partition = slot_no % N_GRID
    remote_rank = (slot_no // N_GRID) % CAP
    owner_dev = slot_no // (CAP * N_GRID)
    global_cell = (partition * CELL_PART + rem_cell).astype(jnp.int32)
    results = interpolate(rem_xyz, jnp.take(corners, global_cell, axis=1), jnp.take(solution, global_cell, axis=1))
    live_count = rem_count[owner_dev, partition]
    is_live = remote_rank < live_count
    rem_values = jnp.where(is_live[None, :], results, 0.0)
    return loc_values, rem_values
```

```python
import functools
import jax
import jax.numpy as jnp
from jax import lax
from jax.experimental import pallas as pl
from jax.experimental.pallas import tpu as pltpu
from jax.sharding import PartitionSpec as P

PASSES = 3
LANES = 128
GROUP = 8 * LANES
ROWS = 64
VMEM_BYTES = 48 << 20


def monomials(corner):
    values = list(corner)
    for bit in (1, 2, 4):
        fresh = list(values)
        for k in range(8):
            if not k & bit:
                fresh[k] = values[k] + values[k | bit]
                fresh[k | bit] = values[k | bit] - values[k]
        values = fresh
    return values


def newton_step(jac, res):
    (a0, a1, a2), (b0, b1, b2), (c0, c1, c2) = jac
    k00 = b1 * c2 - b2 * c1
    k01 = b2 * c0 - b0 * c2
    k02 = b0 * c1 - b1 * c0
    k10 = a2 * c1 - a1 * c2
    k11 = a0 * c2 - a2 * c0
    k12 = a1 * c0 - a0 * c1
    k20 = a1 * b2 - a2 * b1
    k21 = a2 * b0 - a0 * b2
    k22 = a0 * b1 - a1 * b0
    inverse = 1.0 / (a0 * k00 + a1 * k01 + a2 * k02)
    return (
        (k00 * res[0] + k10 * res[1] + k20 * res[2]) * inverse,
        (k01 * res[0] + k11 * res[1] + k21 * res[2]) * inverse,
        (k02 * res[0] + k12 * res[1] + k22 * res[2]) * inverse,
    )


def interpolate(points, value):
    coefs = [monomials([value(8 * i + k) for k in range(8)]) for i in range(3)]
    step = newton_step(
        [[c[1], c[2], c[4]] for c in coefs], [coefs[i][0] - points[i] for i in range(3)]
    )
    xi = [-s for s in step]
    for _ in range(PASSES - 1):
        x, y, z = xi
        jac, res = [], []
        for i in range(3):
            c = coefs[i]
            a0 = c[0] + c[4] * z
            a1 = c[1] + c[5] * z
            a2 = c[2] + c[6] * z
            a3 = c[3] + c[7] * z
            dx = a1 + a3 * y
            dy = a2 + a3 * x
            dz = (c[4] + c[6] * y) + (c[5] + c[7] * y) * x
            jac.append([dx, dy, dz])
            res.append((a0 + a2 * y) + dx * x - points[i])
        step = newton_step(jac, res)
        xi = [xi[d] - step[d] for d in range(3)]
    low = [0.5 - 0.5 * v for v in xi]
    high = [0.5 + 0.5 * v for v in xi]
    plane = [p * q for q in (low[1], high[1]) for p in (low[0], high[0])]
    weights = [w * q for q in (low[2], high[2]) for w in plane]
    outs = []
    for f in range(5):
        total = weights[0] * value(24 + 8 * f)
        for k in range(1, 8):
            total = total + weights[k] * value(24 + 8 * f + k)
        outs.append(total)
    return outs


def request_kernel(xyz_ref, cell_ref, count_ref, out_ref):
    grid, depth, _ = out_ref.shape
    slots = xyz_ref.shape[1]
    width = -(-slots // LANES) * LANES
    wide = lambda a: a if a.shape[1] == width else jnp.pad(a, ((0, 0), (0, width - a.shape[1])))
    stack = jnp.concatenate(
        [
            jnp.zeros((ROWS, width), jnp.float32),
            wide(xyz_ref[...]),
            wide(cell_ref[...].astype(jnp.float32)),
            wide(count_ref[...].astype(jnp.float32)),
            jnp.zeros((LANES - ROWS - 5, width), jnp.float32),
        ],
        0,
    )
    turned = jnp.concatenate(
        [stack[:, k : k + LANES].T for k in range(0, width, LANES)], 0
    )
    counts = turned[0:grid, ROWS + 4 : ROWS + 5]
    lane = lax.broadcasted_iota(jnp.int32, (grid, LANES), 1)
    for c in range(depth):
        live = jnp.where(counts > float(c), 1.0, 0.0)
        out_ref[:, c, :] = jnp.where(lane == ROWS + 4, live, turned[c * grid : (c + 1) * grid, :])


def gather_rows(table_ref, cell, buf, at, base, count):
    for j in range(count):
        buf[pl.ds(at + j, 1), :] = table_ref[pl.ds(cell(base + j), 1), :]


def local_groups(first, last, help_count, table_ref, cell_ref, live_ref, xyz_ref, out_ref, buf, turned, points, outs):
    slots = cell_ref.shape[0]
    slab = slots // help_count
    live = live_ref[0, 0]

    def group(g, _):
        start = pl.multiple_of(g * GROUP, GROUP)

        def block(b, _):
            off = pl.multiple_of(start + b * LANES, LANES)
            gather_rows(table_ref, lambda i: cell_ref[i], buf, 0, off, LANES)
            turned[pl.ds(pl.multiple_of(b * ROWS, ROWS), ROWS), :] = buf[...].T[0:ROWS, :]
            points[pl.ds(pl.multiple_of(b * 8, 8), 3), :] = xyz_ref[:, pl.ds(off, LANES)]
            return 0

        lax.fori_loop(0, 8, block, 0)
        values = interpolate(
            [points[pl.ds(d, 8, stride=8), :] for d in range(3)],
            lambda v: turned[pl.ds(v, 8, stride=ROWS), :],
        )
        slot = (
            start
            + lax.broadcasted_iota(jnp.int32, (8, LANES), 0) * LANES
            + lax.broadcasted_iota(jnp.int32, (8, LANES), 1)
        )
        keep = lax.rem(slot, slab) * help_count + lax.div(slot, slab) < live
        for f in range(5):
            outs[pl.ds(f, 8, stride=8), :] = jnp.where(keep, values[f], 0.0)
        for b in range(8):
            out_ref[:, pl.ds(pl.multiple_of(start + b * LANES, LANES), LANES)] = outs[pl.ds(b * 8, 5), :]
        return 0

    lax.fori_loop(first, last, group, 0)


def first_kernel(last, help_count, _, corners_ref, solution_ref, cell_ref, live_ref, xyz_ref, table_ref, out_ref, buf, turned, points, outs):
    cells = corners_ref.shape[1]

    def chunk(t, _):
        off = pl.multiple_of(t * LANES, LANES)
        both = jnp.concatenate(
            [corners_ref[:, pl.ds(off, LANES)] * 0.125, solution_ref[:, pl.ds(off, LANES)]], 0
        )
        table_ref[pl.ds(off, LANES), 0:ROWS] = both.T
        return 0

    lax.fori_loop(0, cells // LANES, chunk, 0, unroll=4)
    local_groups(0, last, help_count, table_ref, cell_ref, live_ref, xyz_ref, out_ref, buf, turned, points, outs)


def second_kernel(first, help_count, _, table_ref, cell_ref, live_ref, xyz_ref, early_ref, out_ref, buf, turned, points, outs):
    if first:
        out_ref[:, 0 : first * GROUP] = early_ref[...]
    local_groups(first, cell_ref.shape[0] // GROUP, help_count, table_ref, cell_ref, live_ref, xyz_ref, out_ref, buf, turned, points, outs)


def answer_kernel(request_ref, table_ref, out_ref, rows, cells, cell_smem, buf, sem):
    grid, depth, _ = request_ref.shape
    blocks = out_ref.shape[2] // LANES
    mine = lax.axis_index("grid")
    for c in range(depth):
        rows[pl.ds(c * grid, grid), :] = request_ref[:, c, :]
    cells[...] = rows[...].astype(jnp.int32)
    copy = pltpu.make_async_copy(cells, cell_smem, sem)
    copy.start()
    copy.wait()
    lane = lax.broadcasted_iota(jnp.int32, (LANES, LANES), 1)
    short = lane[0:8]
    for k in range(blocks):
        count = min(LANES, grid * depth - k * LANES)
        gather_rows(table_ref, lambda i: cell_smem[i, ROWS + 3], buf, 0, k * LANES, count)
        mixed = jnp.where(lane[0:count] < ROWS, buf[0:count, :], rows[k * LANES : k * LANES + count, :])
        if count < LANES:
            mixed = jnp.concatenate([mixed, jnp.zeros((LANES - count, LANES), jnp.float32)], 0)
        turned = mixed.T
        value = lambda v: turned[v : v + 1, :]
        results = interpolate([value(ROWS + d) for d in range(3)], value)
        keep = value(ROWS + 4) > 0.5
        block = jnp.concatenate(
            [jnp.where(keep, r, 0.0) for r in results] + [jnp.zeros((3, LANES), jnp.float32)], 0
        )
        here = lax.rem(short, grid) == mine

        def reply(r, _):
            moved = pltpu.roll(block, lax.rem(mine - r + LANES, LANES), 1)
            out_ref[r, :, k * LANES : (k + 1) * LANES] = jnp.where(here, moved, 0.0)
            return 0

        lax.fori_loop(0, grid, reply, 0, unroll=min(8, grid))


def per_device(help_count, corners, solution, loc_xyz, loc_cell, loc_live, rem_xyz, rem_cell, rem_count):
    grid = rem_count.shape[1]
    slots = rem_cell.shape[0]
    depth = slots // grid
    cells = corners.shape[1]
    loc = loc_cell.shape[0]
    early = (loc // GROUP) * 3 // 8
    vmem = pl.BlockSpec(memory_space=pltpu.VMEM)
    smem = pl.BlockSpec(memory_space=pltpu.SMEM)
    anyw = pl.BlockSpec(memory_space=pl.ANY)
    params = pltpu.CompilerParams(vmem_limit_bytes=VMEM_BYTES)
    scratch = [
        pltpu.VMEM((LANES, LANES), jnp.float32),
        pltpu.VMEM((8 * ROWS, LANES), jnp.float32),
        pltpu.VMEM((8 * 8, LANES), jnp.float32),
        pltpu.VMEM((8 * 8, LANES), jnp.float32),
    ]

    request = pl.pallas_call(
        request_kernel,
        out_shape=jax.ShapeDtypeStruct((grid, depth, LANES), jnp.float32),
        in_specs=[vmem] * 3,
        out_specs=vmem,
        compiler_params=params,
        name="request",
    )(rem_xyz, rem_cell.reshape(1, slots), rem_count)
    asked = lax.all_to_all(request, "grid", split_axis=0, concat_axis=0, tiled=True)
    table, early_values = pl.pallas_call(
        functools.partial(first_kernel, early, help_count),
        out_shape=(
            pltpu.VMEM((cells, LANES), jnp.float32),
            jax.ShapeDtypeStruct((5, early * GROUP), jnp.float32),
        ),
        in_specs=[anyw, vmem, vmem, smem, smem, vmem],
        out_specs=(vmem, vmem),
        scratch_shapes=scratch,
        compiler_params=params,
        cost_estimate=pl.CostEstimate(flops=1 << 24, bytes_accessed=1 << 24, transcendentals=0),
        name="local_early",
    )(request, corners, solution, loc_cell, loc_live, loc_xyz)
    width = -(-slots // LANES) * LANES
    answers = pl.pallas_call(
        answer_kernel,
        out_shape=jax.ShapeDtypeStruct((grid, 8, width), jnp.float32),
        in_specs=[vmem, vmem],
        out_specs=vmem,
        scratch_shapes=[
            pltpu.VMEM((slots, LANES), jnp.float32),
            pltpu.VMEM((slots, LANES), jnp.int32),
            pltpu.SMEM((slots, LANES), jnp.int32),
            pltpu.VMEM((LANES, LANES), jnp.float32),
            pltpu.SemaphoreType.DMA,
        ],
        compiler_params=params,
        name="answer",
    )(asked, table)
    returned = lax.all_to_all(answers, "grid", split_axis=0, concat_axis=0, tiled=True)
    loc_values = pl.pallas_call(
        functools.partial(second_kernel, early, help_count),
        out_shape=jax.ShapeDtypeStruct((5, loc), jnp.float32),
        in_specs=[anyw, vmem, smem, smem, vmem, vmem],
        out_specs=vmem,
        scratch_shapes=scratch,
        compiler_params=params,
        cost_estimate=pl.CostEstimate(flops=1 << 24, bytes_accessed=1 << 24, transcendentals=0),
        name="local_late",
    )(answers, table, loc_cell, loc_live, loc_xyz, early_values)
    rem_values = jnp.sum(returned, axis=0)[0:5, 0:slots]
    return (loc_values, rem_values)


def solution(mesh):
    placed = (
        P(None, "grid"),
        P(None, "grid"),
        P(None, ("grid", "help")),
        P(("grid", "help")),
        P("grid", "help"),
        P(None, ("grid", "help")),
        P(("grid", "help")),
        P(("grid", "help"), None),
    )
    return jax.shard_map(
        functools.partial(per_device, mesh.shape["help"]),
        mesh=mesh,
        in_specs=placed,
        out_specs=(P(None, ("grid", "help")), P(None, ("grid", "help"))),
        check_vma=False,
    )
```

```python
import functools
import jax
import jax.numpy as jnp
from jax import lax
from jax.experimental import pallas as pl
from jax.experimental.pallas import tpu as pltpu
from jax.sharding import PartitionSpec as P

PASSES = 3
LANES = 128
GROUP = 8 * LANES
ROWS = 64
VMEM_BYTES = 32 << 20
EARLY = 3
LEAD = 3
QUARTERS = 4
STRIDE = 72


def monomials(corner):
    values = list(corner)
    for bit in (1, 2, 4):
        fresh = list(values)
        for k in range(8):
            if not k & bit:
                fresh[k] = values[k] + values[k | bit]
                fresh[k | bit] = values[k | bit] - values[k]
        values = fresh
    return values


def newton_step(jac, res):
    (a0, a1, a2), (b0, b1, b2), (c0, c1, c2) = jac
    k00 = b1 * c2 - b2 * c1
    k01 = b2 * c0 - b0 * c2
    k02 = b0 * c1 - b1 * c0
    k10 = a2 * c1 - a1 * c2
    k11 = a0 * c2 - a2 * c0
    k12 = a1 * c0 - a0 * c1
    k20 = a1 * b2 - a2 * b1
    k21 = a2 * b0 - a0 * b2
    k22 = a0 * b1 - a1 * b0
    inverse = 1.0 / (a0 * k00 + a1 * k01 + a2 * k02)
    return (
        (k00 * res[0] + k10 * res[1] + k20 * res[2]) * inverse,
        (k01 * res[0] + k11 * res[1] + k21 * res[2]) * inverse,
        (k02 * res[0] + k12 * res[1] + k22 * res[2]) * inverse,
    )


def newton(points, coef):
    step = newton_step(
        [[coef(i, 1), coef(i, 2), coef(i, 4)] for i in range(3)],
        [coef(i, 0) - points[i] for i in range(3)],
    )
    xi = [-s for s in step]
    for _ in range(PASSES - 1):
        x, y, z = xi
        jac, res = [], []
        for i in range(3):
            a0 = coef(i, 0) + coef(i, 4) * z
            a1 = coef(i, 1) + coef(i, 5) * z
            a2 = coef(i, 2) + coef(i, 6) * z
            a3 = coef(i, 3) + coef(i, 7) * z
            dx = a1 + a3 * y
            dy = a2 + a3 * x
            dz = (coef(i, 4) + coef(i, 6) * y) + (coef(i, 5) + coef(i, 7) * y) * x
            jac.append([dx, dy, dz])
            res.append((a0 + a2 * y) + dx * x - points[i])
        step = newton_step(jac, res)
        xi = [xi[d] - step[d] for d in range(3)]
    return xi


def blend(xi, value):
    low = [0.5 - 0.5 * v for v in xi]
    high = [0.5 + 0.5 * v for v in xi]
    plane = [p * q for q in (low[1], high[1]) for p in (low[0], high[0])]
    weights = [w * q for q in (low[2], high[2]) for w in plane]
    outs = []
    for f in range(5):
        total = weights[0] * value(24 + 8 * f)
        for k in range(1, 8):
            total = total + weights[k] * value(24 + 8 * f + k)
        outs.append(total)
    return outs


def wait_all(copies):
    for c in copies:
        c.start()
    for c in copies:
        c.wait()


def request_kernel(lead, xyz_hbm, cell_hbm, count_hbm, out_ref, xyz_ref, cell_ref, count_ref, sems):
    wait_all(
        [
            pltpu.make_async_copy(xyz_hbm, xyz_ref, sems.at[0]),
            pltpu.make_async_copy(cell_hbm, cell_ref, sems.at[1]),
            pltpu.make_async_copy(count_hbm, count_ref, sems.at[2]),
        ]
    )
    grid, depth, _ = out_ref.shape
    slots = xyz_ref.shape[1]
    width = -(-slots // LANES) * LANES
    wide = lambda a: a if a.shape[1] == width else jnp.pad(a, ((0, 0), (0, width - a.shape[1])))
    stack = jnp.concatenate(
        [
            jnp.zeros((ROWS, width), jnp.float32),
            wide(xyz_ref[...]),
            wide(cell_ref[...].astype(jnp.float32)),
            wide(count_ref[...].astype(jnp.float32)),
            jnp.zeros((LANES - ROWS - 5, width), jnp.float32),
        ],
        0,
    )
    turned = jnp.concatenate(
        [stack[:, k : k + LANES].T for k in range(0, width, LANES)], 0
    )
    counts = turned[0:grid, ROWS + 4 : ROWS + 5]
    lane = lax.broadcasted_iota(jnp.int32, (grid, LANES), 1)
    for c in range(depth):
        live = jnp.where(counts > float(c), 1.0, 0.0)
        whole = jnp.where(lane == ROWS + 4, live, turned[c * grid : (c + 1) * grid, :])
        out_ref[:, c, :] = jnp.concatenate([whole[lead:], whole[:lead]], 0) if lead else whole


class Local:
    @staticmethod
    def scratch(cells, groups):
        return [
            pltpu.VMEM((cells, LANES), jnp.float32),
            *[pltpu.SMEM((2, LANES), jnp.int32)] * QUARTERS,
            *[pltpu.VMEM((LANES, LANES), jnp.float32)] * QUARTERS,
            pltpu.VMEM(((groups + 1) * 8 * STRIDE, LANES), jnp.float32),
            pltpu.VMEM((24, 8, LANES), jnp.float32),
            pltpu.VMEM((3, 8, LANES), jnp.float32),
            pltpu.VMEM((64, LANES), jnp.float32),
            pltpu.VMEM((64, LANES), jnp.float32),
            pltpu.SemaphoreType.DMA((QUARTERS,)),
        ]

    def __init__(self, first, last, help_count, rows, live, xyz, stage, finished, *scratch):
        self.first, self.last, self.help_count = first, last, help_count
        self.rows, self.live, self.xyz, self.stage, self.finished = rows, live, xyz, stage, finished
        self.wide = scratch[0]
        self.smem, self.buf = scratch[1 : 1 + QUARTERS], scratch[1 + QUARTERS : 1 + 2 * QUARTERS]
        (self.turned, self.coefs, self.xi, self.points, self.outs, self.row_sems) = scratch[1 + 2 * QUARTERS :]

    def fetch(self, q, k):
        return pltpu.make_async_copy(self.rows.at[pl.ds(2 * (QUARTERS * self.first + q), 2), :], self.smem[k], self.row_sems.at[k])

    def turn(self, q, k):
        block = self.buf[k][...].T
        for h in range(2):
            at = pl.multiple_of((2 * q + 8 + h) * STRIDE, 8)
            self.turned[pl.ds(at, ROWS), :] = block[h * ROWS : (h + 1) * ROWS, :]

    def gather(self, k):
        for h in range(2):
            lanes = slice(h * ROWS, (h + 1) * ROWS)
            for j in range(LANES):
                self.buf[k][j : j + 1, lanes] = self.wide[pl.ds(self.smem[k][h, j], 1), lanes]

    def begin(self):
        for k in range(QUARTERS):
            self.fetch(k, k).start()

    def run(self):
        groups = self.last - self.first
        stages = (lambda g: None, self.expand, self.solve, self.fields)

        def group(g, _):
            for k in range(QUARTERS):
                q = QUARTERS * g + k
                self.fetch(q, k).wait()
                self.gather(k)
                stages[k](g - 1)
                self.turn(q - 1, (k - 1) % QUARTERS)

                @pl.when(g + 1 < groups)
                def _():
                    self.fetch(q + QUARTERS, k).start()

            @pl.when(g > 0)
            def _():
                self.finished(g - 1)

            return 0

        lax.fori_loop(0, groups, group, 0)
        self.turn(QUARTERS * groups - 1, QUARTERS - 1)
        for stage in stages:
            stage(groups - 1)
        self.finished(groups - 1)

    def value(self, g, v):
        return self.turned[pl.ds((g + 1) * 8 * STRIDE + v, 8, stride=STRIDE), :]

    def expand(self, g):
        for i in range(3):
            for k, c in enumerate(monomials([self.value(g, 8 * i + k) for k in range(8)])):
                self.coefs[8 * i + k] = c
        for b in range(8):
            at = pl.multiple_of(jnp.maximum(self.first + g, 0) * GROUP + b * LANES, LANES)
            self.points[b * 8 : b * 8 + 3, :] = self.xyz[:, pl.ds(at, LANES)]

    def solve(self, g):
        xi = newton(
            [self.points[pl.ds(d, 8, stride=8), :] for d in range(3)],
            lambda i, k: self.coefs[8 * i + k],
        )
        for d in range(3):
            self.xi[d] = xi[d]

    def fields(self, g):
        values = blend([self.xi[d] for d in range(3)], lambda v: self.value(g, v))
        slab = self.xyz.shape[1] // self.help_count
        slot = (
            (self.first + g) * GROUP
            + lax.broadcasted_iota(jnp.int32, (8, LANES), 0) * LANES
            + lax.broadcasted_iota(jnp.int32, (8, LANES), 1)
        )
        keep = lax.rem(slot, slab) * self.help_count + lax.div(slot, slab) < self.live[...]
        for f in range(5):
            self.outs[pl.ds(f, 8, stride=8), :] = jnp.where(keep, values[f], 0.0)
        for b in range(8):
            at = pl.multiple_of((g + 1) * GROUP + b * LANES, LANES)
            self.stage[:, pl.ds(at, LANES)] = self.outs[b * 8 : b * 8 + 5, :]


PIECES = 4


def first_kernel(last, help_count, _, corners_hbm, solution_hbm, cells_hbm, live_hbm, xyz_hbm, table, rows, live, xyz, stage, corners, solution, cells, live_one, sems, *scratch):
    local = Local(0, last, help_count, rows, live, xyz, stage, lambda g: None, *scratch)
    half = table.shape[0]
    piece = half // PIECES
    pieces = []
    for k in range(PIECES):
        for h in range(2):
            at = pl.ds(h * half + k * piece, piece)
            pieces.append(
                (
                    pltpu.make_async_copy(corners_hbm.at[:, at], corners.at[:, at], sems.at[4 * k + 2 * h]),
                    pltpu.make_async_copy(solution_hbm.at[:, at], solution.at[:, at], sems.at[4 * k + 2 * h + 1]),
                )
            )
    small = [
        pltpu.make_async_copy(cells_hbm, cells, sems.at[4 * PIECES]),
        pltpu.make_async_copy(xyz_hbm, xyz, sems.at[4 * PIECES + 1]),
        pltpu.make_async_copy(live_hbm, live_one, sems.at[4 * PIECES + 2]),
    ]
    for c in [c for pair in pieces for c in pair] + small:
        c.start()
    for k in range(PIECES):
        for c in pieces[2 * k] + pieces[2 * k + 1]:
            c.wait()

        def chunk(t, _):
            low = pl.multiple_of(k * piece + t * LANES, LANES)
            high = pl.multiple_of(half + low, LANES)
            both = jnp.concatenate(
                [
                    corners[:, pl.ds(low, LANES)] * 0.125,
                    solution[:, pl.ds(low, LANES)],
                    corners[:, pl.ds(high, LANES)] * 0.125,
                    solution[:, pl.ds(high, LANES)],
                ],
                0,
            ).T
            table[pl.ds(low, LANES), :] = both
            local.wide[pl.ds(low, LANES), :] = both
            local.wide[pl.ds(high, LANES), :] = pltpu.roll(both, ROWS, 1)
            return 0

        lax.fori_loop(0, piece // LANES, chunk, 0, unroll=min(8, piece // LANES))
    for c in small:
        c.wait()
    whole = cells[...]
    other = jnp.where(whole >= half, whole - half, whole + half)
    odd = lax.rem(lax.broadcasted_iota(jnp.int32, whole.shape, 0), 2) == 1
    rows[...] = jnp.where(odd, other, whole)
    live[...] = jnp.broadcast_to(live_one[...], live.shape)
    local.begin()
    local.run()


def second_kernel(first, last, help_count, _, table, rows, live, xyz, early, loc_hbm, stage, out_sems, *scratch):
    def result(g):
        return pltpu.make_async_copy(
            stage.at[:, pl.ds(pl.multiple_of((g + 1) * GROUP, GROUP), GROUP)],
            loc_hbm.at[:, pl.ds(pl.multiple_of((first + g) * GROUP, GROUP), GROUP)],
            out_sems.at[g],
        )

    part = pl.ds(GROUP, first * GROUP)
    before = pltpu.make_async_copy(early.at[:, part], loc_hbm.at[:, pl.ds(0, first * GROUP)], out_sems.at[last - first])
    before.start()
    local = Local(first, last, help_count, rows, live, xyz, stage, lambda g: result(g).start(), *scratch)
    local.begin()
    half = table.shape[0]

    def chunk(t, _):
        at = pl.multiple_of(t * LANES, LANES)
        both = table[pl.ds(at, LANES), :]
        local.wide[pl.ds(at, LANES), :] = both
        local.wide[pl.ds(pl.multiple_of(half + at, LANES), LANES), :] = pltpu.roll(both, ROWS, 1)
        return 0

    lax.fori_loop(0, half // LANES, chunk, 0, unroll=2)
    local.run()
    before.wait()
    for g in range(last - first):
        result(g).wait()


def answer_kernel(request_ref, table_ref, out_ref, rows, cells, cell_smem, buf, sem):
    grid, depth, _ = request_ref.shape
    half = table_ref.shape[0]
    blocks = out_ref.shape[2] // LANES
    mine = lax.axis_index("grid")
    for c in range(depth):
        rows[pl.ds(c * grid, grid), :] = request_ref[:, c, :]
    number = rows[...].astype(jnp.int32)
    cells[...] = jnp.where(number >= half, number - half, number)
    copy = pltpu.make_async_copy(cells, cell_smem, sem)
    copy.start()
    copy.wait()
    lane = lax.broadcasted_iota(jnp.int32, (LANES, LANES), 1)
    short = lane[0:8]
    for k in range(blocks):
        count = min(LANES, grid * depth - k * LANES)
        for j in range(count):
            buf[j : j + 1, :] = table_ref[pl.ds(cell_smem[k * LANES + j, ROWS + 3], 1), :]
        turned = buf[...].T
        asked = rows[k * LANES : k * LANES + count, :]
        if count < LANES:
            asked = jnp.concatenate([asked, jnp.zeros((LANES - count, LANES), jnp.float32)], 0)
        asked = asked.T[ROWS : ROWS + 8, :]
        upper = asked[3:4, :] >= float(half)
        value = lambda v: jnp.where(upper, turned[ROWS + v : ROWS + v + 1, :], turned[v : v + 1, :])
        coefs = [monomials([value(8 * i + k) for k in range(8)]) for i in range(3)]
        xi = newton([asked[d : d + 1, :] for d in range(3)], lambda i, k: coefs[i][k])
        results = blend(xi, value)
        keep = asked[4:5, :] > 0.5
        block = jnp.concatenate(
            [jnp.where(keep, r, 0.0) for r in results] + [jnp.zeros((3, LANES), jnp.float32)], 0
        )
        here = lax.rem(short, grid) == mine

        def reply(r, _):
            moved = pltpu.roll(block, lax.rem(mine - r + LANES, LANES), 1)
            out_ref[r, :, k * LANES : (k + 1) * LANES] = jnp.where(here, moved, 0.0)
            return 0

        lax.fori_loop(0, grid, reply, 0, unroll=min(8, grid))


def per_device(help_count, corners, solution, loc_xyz, loc_cell, loc_live, rem_xyz, rem_cell, rem_count):
    grid = rem_count.shape[1]
    slots = rem_cell.shape[0]
    depth = slots // grid
    cells = corners.shape[1]
    loc = loc_cell.shape[0]
    early = EARLY
    lead = grid * LEAD // 8
    exchange = functools.partial(
        lax.all_to_all,
        axis_name="grid",
        split_axis=0,
        concat_axis=0,
        axis_index_groups=[[(j + lead) % grid for j in range(grid)]],
        tiled=True,
    )
    vmem = pl.BlockSpec(memory_space=pltpu.VMEM)
    hbm = pl.BlockSpec(memory_space=pltpu.HBM)
    anyw = pl.BlockSpec(memory_space=pl.ANY)
    params = pltpu.CompilerParams(vmem_limit_bytes=VMEM_BYTES)
    far = lambda a: pltpu.with_memory_space_constraint(a, pltpu.HBM)
    corners, solution, loc_xyz, rem_xyz, rem_count = map(far, (corners, solution, loc_xyz, rem_xyz, rem_count))
    cells2d = far(loc_cell.reshape(loc // LANES, LANES))
    rem_cell = far(rem_cell.reshape(1, slots))

    request = pl.pallas_call(
        functools.partial(request_kernel, lead),
        out_shape=jax.ShapeDtypeStruct((grid, depth, LANES), jnp.float32),
        in_specs=[hbm] * 3,
        out_specs=vmem,
        scratch_shapes=[
            pltpu.VMEM((3, slots), jnp.float32),
            pltpu.VMEM((1, slots), jnp.int32),
            pltpu.VMEM((1, grid), jnp.int32),
            pltpu.SemaphoreType.DMA((3,)),
        ],
        compiler_params=params,
        name="request",
    )(rem_xyz, rem_cell, rem_count)
    asked = exchange(request)
    table, rows, live, xyz, loc_early = pl.pallas_call(
        functools.partial(first_kernel, early, help_count),
        out_shape=(
            pltpu.VMEM((cells // 2, LANES), jnp.float32),
            pltpu.VMEM((loc // LANES, LANES), jnp.int32),
            pltpu.VMEM((8, LANES), jnp.int32),
            pltpu.VMEM((3, loc), jnp.float32),
            pltpu.VMEM((5, (early + 1) * GROUP), jnp.float32),
        ),
        in_specs=[anyw] + [hbm] * 5,
        out_specs=(vmem,) * 5,
        scratch_shapes=[
            pltpu.VMEM((24, cells), jnp.float32),
            pltpu.VMEM((40, cells), jnp.float32),
            pltpu.VMEM((loc // LANES, LANES), jnp.int32),
            pltpu.VMEM((1, 1), jnp.int32),
            pltpu.SemaphoreType.DMA((4 * PIECES + 3,)),
            *Local.scratch(cells, early),
        ],
        compiler_params=params,
        cost_estimate=pl.CostEstimate(flops=1 << 24, bytes_accessed=1 << 24, transcendentals=0),
        name="local_early",
    )(request, corners, solution, cells2d, loc_live, loc_xyz)
    width = -(-slots // LANES) * LANES
    answers = pl.pallas_call(
        answer_kernel,
        out_shape=jax.ShapeDtypeStruct((grid, 8, width), jnp.float32),
        in_specs=[vmem, vmem],
        out_specs=vmem,
        scratch_shapes=[
            pltpu.VMEM((slots, LANES), jnp.float32),
            pltpu.VMEM((slots, LANES), jnp.int32),
            pltpu.SMEM((slots, LANES), jnp.int32),
            pltpu.VMEM((LANES, LANES), jnp.float32),
            pltpu.SemaphoreType.DMA,
        ],
        compiler_params=params,
        name="answer",
    )(asked, table)
    returned = exchange(answers)
    late = loc // GROUP - early
    loc_values = pl.pallas_call(
        functools.partial(second_kernel, early, loc // GROUP, help_count),
        out_shape=jax.ShapeDtypeStruct((5, loc), jnp.float32),
        in_specs=[anyw] + [vmem] * 5,
        out_specs=hbm,
        scratch_shapes=[
            pltpu.VMEM((5, (late + 1) * GROUP), jnp.float32),
            pltpu.SemaphoreType.DMA((late + 1,)),
            *Local.scratch(cells, late),
        ],
        compiler_params=params,
        cost_estimate=pl.CostEstimate(flops=1 << 24, bytes_accessed=1 << 24, transcendentals=0),
        name="local_late",
    )(answers, table, rows, live, xyz, loc_early)
    rem_values = jnp.sum(returned, axis=0)[0:5, 0:slots]
    return (loc_values, rem_values)


def solution(mesh):
    placed = (
        P(None, "grid"),
        P(None, "grid"),
        P(None, ("grid", "help")),
        P(("grid", "help")),
        P("grid", "help"),
        P(None, ("grid", "help")),
        P(("grid", "help")),
        P(("grid", "help"), None),
    )
    return jax.shard_map(
        functools.partial(per_device, mesh.shape["help"]),
        mesh=mesh,
        in_specs=placed,
        out_specs=(P(None, ("grid", "help")), P(None, ("grid", "help"))),
        check_vma=False,
    )
```

```python
import functools
import jax
import jax.numpy as jnp
from jax import lax
from jax.experimental import pallas as pl
from jax.experimental.pallas import tpu as pltpu
from jax.sharding import PartitionSpec as P

PASSES = 3
LANES = 128
GROUP = 8 * LANES
ROWS = 64
VMEM_BYTES = 32 << 20
EARLY = 3
LEAD = 3
WIDEN = 16
QUARTERS = 4
STRIDE = 72


def monomials(corner):
    values = list(corner)
    for bit in (1, 2, 4):
        fresh = list(values)
        for k in range(8):
            if not k & bit:
                fresh[k] = values[k] + values[k | bit]
                fresh[k | bit] = values[k | bit] - values[k]
        values = fresh
    return values


def newton_step(jac, res):
    (a0, a1, a2), (b0, b1, b2), (c0, c1, c2) = jac
    k00 = b1 * c2 - b2 * c1
    k01 = b2 * c0 - b0 * c2
    k02 = b0 * c1 - b1 * c0
    k10 = a2 * c1 - a1 * c2
    k11 = a0 * c2 - a2 * c0
    k12 = a1 * c0 - a0 * c1
    k20 = a1 * b2 - a2 * b1
    k21 = a2 * b0 - a0 * b2
    k22 = a0 * b1 - a1 * b0
    inverse = 1.0 / (a0 * k00 + a1 * k01 + a2 * k02)
    return (
        (k00 * res[0] + k10 * res[1] + k20 * res[2]) * inverse,
        (k01 * res[0] + k11 * res[1] + k21 * res[2]) * inverse,
        (k02 * res[0] + k12 * res[1] + k22 * res[2]) * inverse,
    )


def newton(points, coef):
    step = newton_step(
        [[coef(i, 1), coef(i, 2), coef(i, 4)] for i in range(3)],
        [coef(i, 0) - points[i] for i in range(3)],
    )
    xi = [-s for s in step]
    for _ in range(PASSES - 1):
        x, y, z = xi
        jac, res = [], []
        for i in range(3):
            a0 = coef(i, 0) + coef(i, 4) * z
            a1 = coef(i, 1) + coef(i, 5) * z
            a2 = coef(i, 2) + coef(i, 6) * z
            a3 = coef(i, 3) + coef(i, 7) * z
            dx = a1 + a3 * y
            dy = a2 + a3 * x
            dz = (coef(i, 4) + coef(i, 6) * y) + (coef(i, 5) + coef(i, 7) * y) * x
            jac.append([dx, dy, dz])
            res.append((a0 + a2 * y) + dx * x - points[i])
        step = newton_step(jac, res)
        xi = [xi[d] - step[d] for d in range(3)]
    return xi


def blend(xi, value):
    low = [0.5 - 0.5 * v for v in xi]
    high = [0.5 + 0.5 * v for v in xi]
    plane = [p * q for q in (low[1], high[1]) for p in (low[0], high[0])]
    weights = [w * q for q in (low[2], high[2]) for w in plane]
    outs = []
    for f in range(5):
        total = weights[0] * value(24 + 8 * f)
        for k in range(1, 8):
            total = total + weights[k] * value(24 + 8 * f + k)
        outs.append(total)
    return outs


def wait_all(copies):
    for c in copies:
        c.start()
    for c in copies:
        c.wait()


def request_kernel(lead, xyz_hbm, cell_hbm, count_hbm, out_ref, xyz_ref, cell_ref, count_ref, sems):
    wait_all(
        [
            pltpu.make_async_copy(xyz_hbm, xyz_ref, sems.at[0]),
            pltpu.make_async_copy(cell_hbm, cell_ref, sems.at[1]),
            pltpu.make_async_copy(count_hbm, count_ref, sems.at[2]),
        ]
    )
    grid, depth, _ = out_ref.shape
    slots = xyz_ref.shape[1]
    width = -(-slots // LANES) * LANES
    wide = lambda a: a if a.shape[1] == width else jnp.pad(a, ((0, 0), (0, width - a.shape[1])))
    stack = jnp.concatenate(
        [
            jnp.zeros((ROWS, width), jnp.float32),
            wide(xyz_ref[...]),
            wide(cell_ref[...].astype(jnp.float32)),
            wide(count_ref[...].astype(jnp.float32)),
            jnp.zeros((LANES - ROWS - 5, width), jnp.float32),
        ],
        0,
    )
    turned = jnp.concatenate(
        [stack[:, k : k + LANES].T for k in range(0, width, LANES)], 0
    )
    counts = turned[0:grid, ROWS + 4 : ROWS + 5]
    lane = lax.broadcasted_iota(jnp.int32, (grid, LANES), 1)
    for c in range(depth):
        live = jnp.where(counts > float(c), 1.0, 0.0)
        whole = jnp.where(lane == ROWS + 4, live, turned[c * grid : (c + 1) * grid, :])
        out_ref[:, c, :] = jnp.concatenate([whole[lead:], whole[:lead]], 0) if lead else whole


class Local:
    @staticmethod
    def scratch(cells, groups):
        return [
            pltpu.VMEM((cells, LANES), jnp.float32),
            *[pltpu.SMEM((2, LANES), jnp.int32)] * QUARTERS,
            *[pltpu.VMEM((LANES, LANES), jnp.float32)] * QUARTERS,
            pltpu.VMEM(((groups + 1) * 8 * STRIDE, LANES), jnp.float32),
            pltpu.VMEM((24, 8, LANES), jnp.float32),
            pltpu.VMEM((3, 8, LANES), jnp.float32),
            pltpu.VMEM((64, LANES), jnp.float32),
            pltpu.VMEM((64, LANES), jnp.float32),
            pltpu.SemaphoreType.DMA((QUARTERS,)),
        ]

    def __init__(self, first, last, help_count, rows, live, xyz, stage, finished, *scratch):
        self.first, self.last, self.help_count = first, last, help_count
        self.rows, self.live, self.xyz, self.stage, self.finished = rows, live, xyz, stage, finished
        self.wide = scratch[0]
        self.smem, self.buf = scratch[1 : 1 + QUARTERS], scratch[1 + QUARTERS : 1 + 2 * QUARTERS]
        (self.turned, self.coefs, self.xi, self.points, self.outs, self.row_sems) = scratch[1 + 2 * QUARTERS :]

    def fetch(self, q, k):
        return pltpu.make_async_copy(self.rows.at[pl.ds(2 * (QUARTERS * self.first + q), 2), :], self.smem[k], self.row_sems.at[k])

    def turn(self, q, k):
        blocks = [self.buf[k + i][...].T for i in range(2)]
        for i in range(2):
            for h in range(2):
                at = pl.multiple_of((2 * (q + i) + 8 + h) * STRIDE, 8)
                self.turned[pl.ds(at, ROWS), :] = blocks[i][h * ROWS : (h + 1) * ROWS, :]

    def gather(self, k):
        for h in range(2):
            lanes = slice(h * ROWS, (h + 1) * ROWS)
            for j in range(LANES):
                self.buf[k][j : j + 1, lanes] = self.wide[pl.ds(self.smem[k][h, j], 1), lanes]

    def begin(self):
        for k in range(QUARTERS):
            self.fetch(k, k).start()

    def run(self):
        groups = self.last - self.first
        stages = (lambda g: None, self.expand, self.solve, self.fields)

        def group(g, _):
            for k in range(QUARTERS):
                q = QUARTERS * g + k
                self.fetch(q, k).wait()
                self.gather(k)
                stages[k](g - 1)
                if k % 2 == 0:
                    self.turn(q - 2, (k - 2) % QUARTERS)

                @pl.when(g + 1 < groups)
                def _():
                    self.fetch(q + QUARTERS, k).start()

            @pl.when(g > 0)
            def _():
                self.finished(g - 1)

            return 0

        lax.fori_loop(0, groups, group, 0)
        self.turn(QUARTERS * groups - 2, QUARTERS - 2)
        for stage in stages:
            stage(groups - 1)
        self.finished(groups - 1)

    def value(self, g, v):
        return self.turned[pl.ds((g + 1) * 8 * STRIDE + v, 8, stride=STRIDE), :]

    def expand(self, g):
        for i in range(3):
            for k, c in enumerate(monomials([self.value(g, 8 * i + k) for k in range(8)])):
                self.coefs[8 * i + k] = c
        for b in range(8):
            at = pl.multiple_of(jnp.maximum(self.first + g, 0) * GROUP + b * LANES, LANES)
            self.points[b * 8 : b * 8 + 3, :] = self.xyz[:, pl.ds(at, LANES)]

    def solve(self, g):
        xi = newton(
            [self.points[pl.ds(d, 8, stride=8), :] for d in range(3)],
            lambda i, k: self.coefs[8 * i + k],
        )
        for d in range(3):
            self.xi[d] = xi[d]

    def fields(self, g):
        values = blend([self.xi[d] for d in range(3)], lambda v: self.value(g, v))
        slab = self.xyz.shape[1] // self.help_count
        slot = (
            (self.first + g) * GROUP
            + lax.broadcasted_iota(jnp.int32, (8, LANES), 0) * LANES
            + lax.broadcasted_iota(jnp.int32, (8, LANES), 1)
        )
        keep = lax.rem(slot, slab) * self.help_count + lax.div(slot, slab) < self.live[...]
        for f in range(5):
            self.outs[pl.ds(f, 8, stride=8), :] = jnp.where(keep, values[f], 0.0)
        for b in range(8):
            at = pl.multiple_of((g + 1) * GROUP + b * LANES, LANES)
            self.stage[:, pl.ds(at, LANES)] = self.outs[b * 8 : b * 8 + 5, :]


PIECES = 2


def first_kernel(last, help_count, _, corners_hbm, solution_hbm, cells_hbm, live_hbm, xyz_hbm, table, rows, live, xyz, stage, corners, solution, cells, live_one, sems, *scratch):
    local = Local(0, last, help_count, rows, live, xyz, stage, lambda g: None, *scratch)
    half = table.shape[0]
    piece = half // PIECES
    pieces = []
    for k in range(PIECES):
        for h in range(2):
            at = pl.ds(h * half + k * piece, piece)
            pieces.append(
                (
                    pltpu.make_async_copy(corners_hbm.at[:, at], corners.at[:, at], sems.at[4 * k + 2 * h]),
                    pltpu.make_async_copy(solution_hbm.at[:, at], solution.at[:, at], sems.at[4 * k + 2 * h + 1]),
                )
            )
    small = [
        pltpu.make_async_copy(cells_hbm, cells, sems.at[4 * PIECES]),
        pltpu.make_async_copy(xyz_hbm, xyz, sems.at[4 * PIECES + 1]),
        pltpu.make_async_copy(live_hbm, live_one, sems.at[4 * PIECES + 2]),
    ]
    for c in small[:1] + [c for pair in pieces for c in pair] + small[1:]:
        c.start()
    small[0].wait()
    whole = cells[...]
    other = jnp.where(whole >= half, whole - half, whole + half)
    odd = lax.rem(lax.broadcasted_iota(jnp.int32, whole.shape, 0), 2) == 1
    rows[...] = jnp.where(odd, other, whole)
    local.begin()
    for k in range(PIECES):
        for c in pieces[2 * k] + pieces[2 * k + 1]:
            c.wait()

        def chunk(t, _):
            low = pl.multiple_of(k * piece + t * LANES, LANES)
            high = pl.multiple_of(half + low, LANES)
            both = jnp.concatenate(
                [
                    corners[:, pl.ds(low, LANES)] * 0.125,
                    solution[:, pl.ds(low, LANES)],
                    corners[:, pl.ds(high, LANES)] * 0.125,
                    solution[:, pl.ds(high, LANES)],
                ],
                0,
            ).T
            table[pl.ds(low, LANES), :] = both
            local.wide[pl.ds(low, LANES), :] = both
            local.wide[pl.ds(high, LANES), :] = pltpu.roll(both, ROWS, 1)
            return 0

        lax.fori_loop(0, piece // LANES, chunk, 0, unroll=min(16, piece // LANES))
    for c in small[1:]:
        c.wait()
    live[...] = jnp.broadcast_to(live_one[...], live.shape)
    local.run()


def second_kernel(first, last, help_count, _, table, rows, live, xyz, early, loc_hbm, stage, out_sem, *scratch):
    before = pltpu.make_async_copy(
        early.at[:, pl.ds(GROUP, first * GROUP)], loc_hbm.at[:, pl.ds(0, first * GROUP)], out_sem
    )
    before.start()
    local = Local(first, last, help_count, rows, live, xyz, stage, lambda g: None, *scratch)
    local.begin()
    half = table.shape[0]

    def chunk(t, _):
        at = pl.multiple_of(t * LANES, LANES)
        both = table[pl.ds(at, LANES), :]
        local.wide[pl.ds(at, LANES), :] = both
        local.wide[pl.ds(pl.multiple_of(half + at, LANES), LANES), :] = pltpu.roll(both, ROWS, 1)
        return 0

    lax.fori_loop(0, half // LANES, chunk, 0, unroll=WIDEN)
    local.run()
    before.wait()


def final_kernel(first, _, stage, returned, before_hbm, loc_hbm, rem_hbm, total, sems):
    loc = pltpu.make_async_copy(
        stage.at[:, pl.ds(GROUP, stage.shape[1] - GROUP)],
        loc_hbm.at[:, pl.ds(first * GROUP, stage.shape[1] - GROUP)],
        sems.at[0],
    )
    loc.start()
    total[...] = jnp.sum(returned[...], axis=0)[0:5, 0 : total.shape[1]]
    rem = pltpu.make_async_copy(total, rem_hbm, sems.at[1])
    rem.start()
    loc.wait()
    rem.wait()


def answer_kernel(request_ref, table_ref, out_ref, rows, cells, cell_smem, buf, sem):
    grid, depth, _ = request_ref.shape
    half = table_ref.shape[0]
    blocks = out_ref.shape[2] // LANES
    mine = lax.axis_index("grid")
    for c in range(depth):
        rows[pl.ds(c * grid, grid), :] = request_ref[:, c, :]
    asked_all = []
    for k in range(blocks):
        count = min(LANES, grid * depth - k * LANES)
        asked = rows[k * LANES : k * LANES + count, :]
        if count < LANES:
            asked = jnp.concatenate([asked, jnp.zeros((LANES - count, LANES), jnp.float32)], 0)
        asked_all.append(asked.T[ROWS : ROWS + 8, :])
        number = asked_all[k][3:4, :].astype(jnp.int32)
        cells[k : k + 1, :] = jnp.where(number >= half, number - half, number)
    copy = pltpu.make_async_copy(cells, cell_smem, sem)
    copy.start()
    copy.wait()
    lane = lax.broadcasted_iota(jnp.int32, (8, LANES), 1)
    for k in range(blocks):
        for j in range(min(LANES, grid * depth - k * LANES)):
            buf[j : j + 1, :] = table_ref[pl.ds(cell_smem[k, j], 1), :]
        turned = buf[...].T
        asked = asked_all[k]
        upper = asked[3:4, :] >= float(half)
        value = lambda v: jnp.where(upper, turned[ROWS + v : ROWS + v + 1, :], turned[v : v + 1, :])
        coefs = [monomials([value(8 * i + k) for k in range(8)]) for i in range(3)]
        xi = newton([asked[d : d + 1, :] for d in range(3)], lambda i, k: coefs[i][k])
        results = blend(xi, value)
        keep = asked[4:5, :] > 0.5
        block = jnp.concatenate(
            [jnp.where(keep, r, 0.0) for r in results] + [jnp.zeros((3, LANES), jnp.float32)], 0
        )
        here = lax.rem(lane, grid) == mine

        def reply(r, _):
            moved = pltpu.roll(block, lax.rem(mine - r + LANES, LANES), 1)
            out_ref[r, :, k * LANES : (k + 1) * LANES] = jnp.where(here, moved, 0.0)
            return 0

        lax.fori_loop(0, grid, reply, 0, unroll=min(8, grid))


def per_device(help_count, corners, solution, loc_xyz, loc_cell, loc_live, rem_xyz, rem_cell, rem_count):
    grid = rem_count.shape[1]
    slots = rem_cell.shape[0]
    depth = slots // grid
    cells = corners.shape[1]
    loc = loc_cell.shape[0]
    early = EARLY
    lead = grid * LEAD // 8
    exchange = functools.partial(
        lax.all_to_all,
        axis_name="grid",
        split_axis=0,
        concat_axis=0,
        axis_index_groups=[[(j + lead) % grid for j in range(grid)]],
        tiled=True,
    )
    vmem = pl.BlockSpec(memory_space=pltpu.VMEM)
    hbm = pl.BlockSpec(memory_space=pltpu.HBM)
    anyw = pl.BlockSpec(memory_space=pl.ANY)
    params = pltpu.CompilerParams(vmem_limit_bytes=VMEM_BYTES)
    far = lambda a: pltpu.with_memory_space_constraint(a, pltpu.HBM)
    corners, solution, loc_xyz, rem_xyz, rem_count = map(far, (corners, solution, loc_xyz, rem_xyz, rem_count))
    cells2d = far(loc_cell.reshape(loc // LANES, LANES))
    rem_cell = far(rem_cell.reshape(1, slots))

    request = pl.pallas_call(
        functools.partial(request_kernel, lead),
        out_shape=jax.ShapeDtypeStruct((grid, depth, LANES), jnp.float32),
        in_specs=[hbm] * 3,
        out_specs=vmem,
        scratch_shapes=[
            pltpu.VMEM((3, slots), jnp.float32),
            pltpu.VMEM((1, slots), jnp.int32),
            pltpu.VMEM((1, grid), jnp.int32),
            pltpu.SemaphoreType.DMA((3,)),
        ],
        compiler_params=params,
        name="request",
    )(rem_xyz, rem_cell, rem_count)
    asked = exchange(request)
    table, rows, live, xyz, loc_early = pl.pallas_call(
        functools.partial(first_kernel, early, help_count),
        out_shape=(
            pltpu.VMEM((cells // 2, LANES), jnp.float32),
            pltpu.VMEM((loc // LANES, LANES), jnp.int32),
            pltpu.VMEM((8, LANES), jnp.int32),
            pltpu.VMEM((3, loc), jnp.float32),
            pltpu.VMEM((5, (early + 1) * GROUP), jnp.float32),
        ),
        in_specs=[anyw] + [hbm] * 5,
        out_specs=(vmem,) * 5,
        scratch_shapes=[
            pltpu.VMEM((24, cells), jnp.float32),
            pltpu.VMEM((40, cells), jnp.float32),
            pltpu.VMEM((loc // LANES, LANES), jnp.int32),
            pltpu.VMEM((1, 1), jnp.int32),
            pltpu.SemaphoreType.DMA((4 * PIECES + 3,)),
            *Local.scratch(cells, early),
        ],
        compiler_params=params,
        cost_estimate=pl.CostEstimate(flops=1 << 24, bytes_accessed=1 << 24, transcendentals=0),
        name="local_early",
    )(request, corners, solution, cells2d, loc_live, loc_xyz)
    width = -(-slots // LANES) * LANES
    answers = pl.pallas_call(
        answer_kernel,
        out_shape=jax.ShapeDtypeStruct((grid, 8, width), jnp.float32),
        in_specs=[vmem, vmem],
        out_specs=vmem,
        scratch_shapes=[
            pltpu.VMEM((slots, LANES), jnp.float32),
            pltpu.VMEM((width // LANES, LANES), jnp.int32),
            pltpu.SMEM((width // LANES, LANES), jnp.int32),
            pltpu.VMEM((LANES, LANES), jnp.float32),
            pltpu.SemaphoreType.DMA,
        ],
        compiler_params=params,
        name="answer",
    )(asked, table)
    returned = exchange(answers)
    late = loc // GROUP - early
    loc_part, stage = pl.pallas_call(
        functools.partial(second_kernel, early, loc // GROUP, help_count),
        out_shape=(
            jax.ShapeDtypeStruct((5, loc), jnp.float32),
            pltpu.VMEM((5, (late + 1) * GROUP), jnp.float32),
        ),
        in_specs=[anyw] + [vmem] * 5,
        out_specs=(hbm, vmem),
        scratch_shapes=[pltpu.SemaphoreType.DMA, *Local.scratch(cells, late)],
        compiler_params=params,
        cost_estimate=pl.CostEstimate(flops=1 << 24, bytes_accessed=1 << 24, transcendentals=0),
        name="local_late",
    )(answers, table, rows, live, xyz, loc_early)
    loc_values, rem_values = pl.pallas_call(
        functools.partial(final_kernel, early),
        out_shape=(
            jax.ShapeDtypeStruct((5, loc), jnp.float32),
            jax.ShapeDtypeStruct((5, slots), jnp.float32),
        ),
        in_specs=[anyw, vmem, vmem, hbm],
        out_specs=(hbm, hbm),
        scratch_shapes=[pltpu.VMEM((5, slots), jnp.float32), pltpu.SemaphoreType.DMA((2,))],
        input_output_aliases={3: 0},
        compiler_params=params,
        name="final",
    )(live, stage, returned, loc_part)
    return (loc_values, rem_values)


def solution(mesh):
    placed = (
        P(None, "grid"),
        P(None, "grid"),
        P(None, ("grid", "help")),
        P(("grid", "help")),
        P("grid", "help"),
        P(None, ("grid", "help")),
        P(("grid", "help")),
        P(("grid", "help"), None),
    )
    return jax.shard_map(
        functools.partial(per_device, mesh.shape["help"]),
        mesh=mesh,
        in_specs=placed,
        out_specs=(P(None, ("grid", "help")), P(None, ("grid", "help"))),
        check_vma=False,
    )
```

```python
import functools
import jax
import jax.numpy as jnp
from jax import lax
from jax.experimental import pallas as pl
from jax.experimental.pallas import tpu as pltpu
from jax.sharding import PartitionSpec as P

PASSES = 3
LANES = 128
GROUP = 8 * LANES
ROWS = 64
VMEM_BYTES = 32 << 20
EARLY = 3
LEAD = 4
WIDEN = 16
QUARTERS = 4
STRIDE = 72


def monomials(corner):
    values = list(corner)
    for bit in (1, 2, 4):
        fresh = list(values)
        for k in range(8):
            if not k & bit:
                fresh[k] = values[k] + values[k | bit]
                fresh[k | bit] = values[k | bit] - values[k]
        values = fresh
    return values


def newton_step(jac, res):
    (a0, a1, a2), (b0, b1, b2), (c0, c1, c2) = jac
    k00 = b1 * c2 - b2 * c1
    k01 = b2 * c0 - b0 * c2
    k02 = b0 * c1 - b1 * c0
    k10 = a2 * c1 - a1 * c2
    k11 = a0 * c2 - a2 * c0
    k12 = a1 * c0 - a0 * c1
    k20 = a1 * b2 - a2 * b1
    k21 = a2 * b0 - a0 * b2
    k22 = a0 * b1 - a1 * b0
    inverse = 1.0 / (a0 * k00 + a1 * k01 + a2 * k02)
    return (
        (k00 * res[0] + k10 * res[1] + k20 * res[2]) * inverse,
        (k01 * res[0] + k11 * res[1] + k21 * res[2]) * inverse,
        (k02 * res[0] + k12 * res[1] + k22 * res[2]) * inverse,
    )


def newton(points, coef):
    step = newton_step(
        [[coef(i, 1), coef(i, 2), coef(i, 4)] for i in range(3)],
        [coef(i, 0) - points[i] for i in range(3)],
    )
    xi = [-s for s in step]
    for _ in range(PASSES - 1):
        x, y, z = xi
        jac, res = [], []
        for i in range(3):
            a0 = coef(i, 0) + coef(i, 4) * z
            a1 = coef(i, 1) + coef(i, 5) * z
            a2 = coef(i, 2) + coef(i, 6) * z
            a3 = coef(i, 3) + coef(i, 7) * z
            dx = a1 + a3 * y
            dy = a2 + a3 * x
            dz = (coef(i, 4) + coef(i, 6) * y) + (coef(i, 5) + coef(i, 7) * y) * x
            jac.append([dx, dy, dz])
            res.append((a0 + a2 * y) + dx * x - points[i])
        step = newton_step(jac, res)
        xi = [xi[d] - step[d] for d in range(3)]
    return xi


def blend(xi, value):
    low = [0.5 - 0.5 * v for v in xi]
    high = [0.5 + 0.5 * v for v in xi]
    plane = [p * q for q in (low[1], high[1]) for p in (low[0], high[0])]
    weights = [w * q for q in (low[2], high[2]) for w in plane]
    outs = []
    for f in range(5):
        total = weights[0] * value(24 + 8 * f)
        for k in range(1, 8):
            total = total + weights[k] * value(24 + 8 * f + k)
        outs.append(total)
    return outs


def wait_all(copies):
    for c in copies:
        c.start()
    for c in copies:
        c.wait()


def request_kernel(lead, xyz_hbm, cell_hbm, count_hbm, out_ref, xyz_ref, cell_ref, count_ref, sems):
    wait_all(
        [
            pltpu.make_async_copy(xyz_hbm, xyz_ref, sems.at[0]),
            pltpu.make_async_copy(cell_hbm, cell_ref, sems.at[1]),
            pltpu.make_async_copy(count_hbm, count_ref, sems.at[2]),
        ]
    )
    grid, depth, _ = out_ref.shape
    slots = xyz_ref.shape[1]
    width = -(-slots // LANES) * LANES
    wide = lambda a: a if a.shape[1] == width else jnp.pad(a, ((0, 0), (0, width - a.shape[1])))
    stack = jnp.concatenate(
        [
            jnp.zeros((ROWS, width), jnp.float32),
            wide(xyz_ref[...]),
            wide(cell_ref[...].astype(jnp.float32)),
            wide(count_ref[...].astype(jnp.float32)),
            jnp.zeros((LANES - ROWS - 5, width), jnp.float32),
        ],
        0,
    )
    turned = jnp.concatenate(
        [stack[:, k : k + LANES].T for k in range(0, width, LANES)], 0
    )
    counts = turned[0:grid, ROWS + 4 : ROWS + 5]
    lane = lax.broadcasted_iota(jnp.int32, (grid, LANES), 1)
    for c in range(depth):
        live = jnp.where(counts > float(c), 1.0, 0.0)
        whole = jnp.where(lane == ROWS + 4, live, turned[c * grid : (c + 1) * grid, :])
        out_ref[:, c, :] = jnp.concatenate([whole[lead:], whole[:lead]], 0) if lead else whole


class Local:
    @staticmethod
    def scratch(cells, groups):
        return [
            pltpu.VMEM((cells, LANES), jnp.float32),
            *[pltpu.SMEM((2, LANES), jnp.int32)] * QUARTERS,
            *[pltpu.VMEM((LANES, LANES), jnp.float32)] * QUARTERS,
            pltpu.VMEM(((groups + 1) * 8 * STRIDE, LANES), jnp.float32),
            pltpu.VMEM((24, 8, LANES), jnp.float32),
            pltpu.VMEM((3, 8, LANES), jnp.float32),
            pltpu.VMEM((64, LANES), jnp.float32),
            pltpu.VMEM((64, LANES), jnp.float32),
            pltpu.SemaphoreType.DMA((QUARTERS,)),
        ]

    def __init__(self, first, last, help_count, rows, live, xyz, stage, finished, *scratch):
        self.first, self.last, self.help_count = first, last, help_count
        self.rows, self.live, self.xyz, self.stage, self.finished = rows, live, xyz, stage, finished
        self.wide = scratch[0]
        self.smem, self.buf = scratch[1 : 1 + QUARTERS], scratch[1 + QUARTERS : 1 + 2 * QUARTERS]
        (self.turned, self.coefs, self.xi, self.points, self.outs, self.row_sems) = scratch[1 + 2 * QUARTERS :]

    def fetch(self, q, k):
        return pltpu.make_async_copy(self.rows.at[pl.ds(2 * (QUARTERS * self.first + q), 2), :], self.smem[k], self.row_sems.at[k])

    def turn(self, q, k):
        blocks = [self.buf[k + i][...].T for i in range(2)]
        for i in range(2):
            for h in range(2):
                at = pl.multiple_of((2 * (q + i) + 8 + h) * STRIDE, 8)
                self.turned[pl.ds(at, ROWS), :] = blocks[i][h * ROWS : (h + 1) * ROWS, :]

    def gather(self, k):
        for h in range(2):
            lanes = slice(h * ROWS, (h + 1) * ROWS)
            for j in range(LANES):
                self.buf[k][j : j + 1, lanes] = self.wide[pl.ds(self.smem[k][h, j], 1), lanes]

    def begin(self):
        for k in range(QUARTERS):
            self.fetch(k, k).start()

    def run(self):
        groups = self.last - self.first
        stages = (lambda g: None, self.expand, self.solve, self.fields)

        def group(g, _):
            for k in range(QUARTERS):
                q = QUARTERS * g + k
                self.fetch(q, k).wait()
                self.gather(k)
                stages[k](g - 1)
                if k % 2 == 0:
                    self.turn(q - 2, (k - 2) % QUARTERS)

                @pl.when(g + 1 < groups)
                def _():
                    self.fetch(q + QUARTERS, k).start()

            @pl.when(g > 0)
            def _():
                self.finished(g - 1)

            return 0

        lax.fori_loop(0, groups, group, 0)
        self.turn(QUARTERS * groups - 2, QUARTERS - 2)
        for stage in stages:
            stage(groups - 1)
        self.finished(groups - 1)

    def value(self, g, v):
        return self.turned[pl.ds((g + 1) * 8 * STRIDE + v, 8, stride=STRIDE), :]

    def expand(self, g):
        for i in range(3):
            for k, c in enumerate(monomials([self.value(g, 8 * i + k) for k in range(8)])):
                self.coefs[8 * i + k] = c
        for b in range(8):
            at = pl.multiple_of(jnp.maximum(self.first + g, 0) * GROUP + b * LANES, LANES)
            self.points[b * 8 : b * 8 + 3, :] = self.xyz[:, pl.ds(at, LANES)]

    def solve(self, g):
        xi = newton(
            [self.points[pl.ds(d, 8, stride=8), :] for d in range(3)],
            lambda i, k: self.coefs[8 * i + k],
        )
        for d in range(3):
            self.xi[d] = xi[d]

    def fields(self, g):
        values = blend([self.xi[d] for d in range(3)], lambda v: self.value(g, v))
        slab = self.xyz.shape[1] // self.help_count
        slot = (
            (self.first + g) * GROUP
            + lax.broadcasted_iota(jnp.int32, (8, LANES), 0) * LANES
            + lax.broadcasted_iota(jnp.int32, (8, LANES), 1)
        )
        keep = lax.rem(slot, slab) * self.help_count + lax.div(slot, slab) < self.live[...]
        for f in range(5):
            self.outs[pl.ds(f, 8, stride=8), :] = jnp.where(keep, values[f], 0.0)
        for b in range(8):
            at = pl.multiple_of((g + 1) * GROUP + b * LANES, LANES)
            self.stage[:, pl.ds(at, LANES)] = self.outs[b * 8 : b * 8 + 5, :]


PIECES = 2


def first_kernel(last, help_count, _, corners_hbm, solution_hbm, cells_hbm, live_hbm, xyz_hbm, table, rows, live, xyz, stage, corners, solution, cells, live_one, sems, *scratch):
    local = Local(0, last, help_count, rows, live, xyz, stage, lambda g: None, *scratch)
    half = table.shape[0]
    piece = half // PIECES
    pieces = []
    for k in range(PIECES):
        for h in range(2):
            at = pl.ds(h * half + k * piece, piece)
            pieces.append(
                (
                    pltpu.make_async_copy(corners_hbm.at[:, at], corners.at[:, at], sems.at[4 * k + 2 * h]),
                    pltpu.make_async_copy(solution_hbm.at[:, at], solution.at[:, at], sems.at[4 * k + 2 * h + 1]),
                )
            )
    small = [
        pltpu.make_async_copy(cells_hbm, cells, sems.at[4 * PIECES]),
        pltpu.make_async_copy(xyz_hbm, xyz, sems.at[4 * PIECES + 1]),
        pltpu.make_async_copy(live_hbm, live_one, sems.at[4 * PIECES + 2]),
    ]
    for c in small[:1] + [c for pair in pieces for c in pair] + small[1:]:
        c.start()
    small[0].wait()
    whole = cells[...]
    other = jnp.where(whole >= half, whole - half, whole + half)
    odd = lax.rem(lax.broadcasted_iota(jnp.int32, whole.shape, 0), 2) == 1
    rows[...] = jnp.where(odd, other, whole)
    local.begin()
    for k in range(PIECES):
        for c in pieces[2 * k] + pieces[2 * k + 1]:
            c.wait()

        def chunk(t, _):
            low = pl.multiple_of(k * piece + t * LANES, LANES)
            high = pl.multiple_of(half + low, LANES)
            both = jnp.concatenate(
                [
                    corners[:, pl.ds(low, LANES)] * 0.125,
                    solution[:, pl.ds(low, LANES)],
                    corners[:, pl.ds(high, LANES)] * 0.125,
                    solution[:, pl.ds(high, LANES)],
                ],
                0,
            ).T
            table[pl.ds(low, LANES), :] = both
            local.wide[pl.ds(low, LANES), :] = both
            local.wide[pl.ds(high, LANES), :] = pltpu.roll(both, ROWS, 1)
            return 0

        lax.fori_loop(0, piece // LANES, chunk, 0, unroll=min(16, piece // LANES))
    for c in small[1:]:
        c.wait()
    live[...] = jnp.broadcast_to(live_one[...], live.shape)
    local.run()


def second_kernel(first, last, help_count, _, table, rows, live, xyz, early, loc_hbm, stage, out_sem, *scratch):
    before = pltpu.make_async_copy(
        early.at[:, pl.ds(GROUP, first * GROUP)], loc_hbm.at[:, pl.ds(0, first * GROUP)], out_sem
    )
    before.start()
    local = Local(first, last, help_count, rows, live, xyz, stage, lambda g: None, *scratch)
    local.begin()
    half = table.shape[0]

    def chunk(t, _):
        at = pl.multiple_of(t * LANES, LANES)
        both = table[pl.ds(at, LANES), :]
        local.wide[pl.ds(at, LANES), :] = both
        local.wide[pl.ds(pl.multiple_of(half + at, LANES), LANES), :] = pltpu.roll(both, ROWS, 1)
        return 0

    lax.fori_loop(0, half // LANES, chunk, 0, unroll=WIDEN)
    local.run()
    before.wait()


def final_kernel(first, _, stage, returned, before_hbm, loc_hbm, rem_hbm, total, sems):
    loc = pltpu.make_async_copy(
        stage.at[:, pl.ds(GROUP, stage.shape[1] - GROUP)],
        loc_hbm.at[:, pl.ds(first * GROUP, stage.shape[1] - GROUP)],
        sems.at[0],
    )
    loc.start()
    total[...] = jnp.sum(returned[...], axis=0)[0:5, 0 : total.shape[1]]
    rem = pltpu.make_async_copy(total, rem_hbm, sems.at[1])
    rem.start()
    loc.wait()
    rem.wait()


def answer_kernel(request_ref, table_ref, out_ref, rows, buf):
    grid, depth, _ = request_ref.shape
    half = table_ref.shape[0]
    blocks = out_ref.shape[2] // LANES
    mine = lax.axis_index("grid")
    for c in range(depth):
        rows[pl.ds(c * grid, grid), :] = request_ref[:, c, :]
    asked_all, cells = [], []
    for k in range(blocks):
        count = min(LANES, grid * depth - k * LANES)
        asked = rows[k * LANES : k * LANES + count, :]
        if count < LANES:
            asked = jnp.concatenate([asked, jnp.zeros((LANES - count, LANES), jnp.float32)], 0)
        asked_all.append(asked.T[ROWS : ROWS + 8, :])
        number = asked_all[k][3:4, :].astype(jnp.int32)
        cells.append(jnp.where(number >= half, number - half, number))
    lane = lax.broadcasted_iota(jnp.int32, (8, LANES), 1)
    for k in range(blocks):
        for j in range(min(LANES, grid * depth - k * LANES)):
            buf[j : j + 1, :] = table_ref[pl.ds(cells[k][0, j], 1), :]
        turned = buf[...].T
        asked = asked_all[k]
        upper = asked[3:4, :] >= float(half)
        value = lambda v: jnp.where(upper, turned[ROWS + v : ROWS + v + 1, :], turned[v : v + 1, :])
        coefs = [monomials([value(8 * i + k) for k in range(8)]) for i in range(3)]
        xi = newton([asked[d : d + 1, :] for d in range(3)], lambda i, k: coefs[i][k])
        results = blend(xi, value)
        keep = asked[4:5, :] > 0.5
        block = jnp.concatenate(
            [jnp.where(keep, r, 0.0) for r in results] + [jnp.zeros((3, LANES), jnp.float32)], 0
        )
        here = lax.rem(lane, grid) == mine

        def reply(r, _):
            moved = pltpu.roll(block, lax.rem(mine - r + LANES, LANES), 1)
            out_ref[r, :, k * LANES : (k + 1) * LANES] = jnp.where(here, moved, 0.0)
            return 0

        lax.fori_loop(0, grid, reply, 0, unroll=min(8, grid))


def per_device(help_count, corners, solution, loc_xyz, loc_cell, loc_live, rem_xyz, rem_cell, rem_count):
    grid = rem_count.shape[1]
    slots = rem_cell.shape[0]
    depth = slots // grid
    cells = corners.shape[1]
    loc = loc_cell.shape[0]
    early = EARLY
    lead = grid * LEAD // 8
    exchange = functools.partial(
        lax.all_to_all,
        axis_name="grid",
        split_axis=0,
        concat_axis=0,
        axis_index_groups=[[(j + lead) % grid for j in range(grid)]],
        tiled=True,
    )
    vmem = pl.BlockSpec(memory_space=pltpu.VMEM)
    hbm = pl.BlockSpec(memory_space=pltpu.HBM)
    anyw = pl.BlockSpec(memory_space=pl.ANY)
    params = pltpu.CompilerParams(vmem_limit_bytes=VMEM_BYTES)
    far = lambda a: pltpu.with_memory_space_constraint(a, pltpu.HBM)
    corners, solution, loc_xyz, rem_xyz, rem_count = map(far, (corners, solution, loc_xyz, rem_xyz, rem_count))
    cells2d = far(loc_cell.reshape(loc // LANES, LANES))
    rem_cell = far(rem_cell.reshape(1, slots))

    request = pl.pallas_call(
        functools.partial(request_kernel, lead),
        out_shape=jax.ShapeDtypeStruct((grid, depth, LANES), jnp.float32),
        in_specs=[hbm] * 3,
        out_specs=vmem,
        scratch_shapes=[
            pltpu.VMEM((3, slots), jnp.float32),
            pltpu.VMEM((1, slots), jnp.int32),
            pltpu.VMEM((1, grid), jnp.int32),
            pltpu.SemaphoreType.DMA((3,)),
        ],
        compiler_params=params,
        name="request",
    )(rem_xyz, rem_cell, rem_count)
    asked = exchange(request)
    table, rows, live, xyz, loc_early = pl.pallas_call(
        functools.partial(first_kernel, early, help_count),
        out_shape=(
            pltpu.VMEM((cells // 2, LANES), jnp.float32),
            pltpu.VMEM((loc // LANES, LANES), jnp.int32),
            pltpu.VMEM((8, LANES), jnp.int32),
            pltpu.VMEM((3, loc), jnp.float32),
            pltpu.VMEM((5, (early + 1) * GROUP), jnp.float32),
        ),
        in_specs=[anyw] + [hbm] * 5,
        out_specs=(vmem,) * 5,
        scratch_shapes=[
            pltpu.VMEM((24, cells), jnp.float32),
            pltpu.VMEM((40, cells), jnp.float32),
            pltpu.VMEM((loc // LANES, LANES), jnp.int32),
            pltpu.VMEM((1, 1), jnp.int32),
            pltpu.SemaphoreType.DMA((4 * PIECES + 3,)),
            *Local.scratch(cells, early),
        ],
        compiler_params=params,
        cost_estimate=pl.CostEstimate(flops=1 << 24, bytes_accessed=1 << 24, transcendentals=0),
        name="local_early",
    )(request, corners, solution, cells2d, loc_live, loc_xyz)
    width = -(-slots // LANES) * LANES
    answers = pl.pallas_call(
        answer_kernel,
        out_shape=jax.ShapeDtypeStruct((grid, 8, width), jnp.float32),
        in_specs=[vmem, vmem],
        out_specs=vmem,
        scratch_shapes=[
            pltpu.VMEM((slots, LANES), jnp.float32),
            pltpu.VMEM((LANES, LANES), jnp.float32),
        ],
        compiler_params=params,
        name="answer",
    )(asked, table)
    returned = exchange(answers)
    late = loc // GROUP - early
    loc_part, stage = pl.pallas_call(
        functools.partial(second_kernel, early, loc // GROUP, help_count),
        out_shape=(
            jax.ShapeDtypeStruct((5, loc), jnp.float32),
            pltpu.VMEM((5, (late + 1) * GROUP), jnp.float32),
        ),
        in_specs=[anyw] + [vmem] * 5,
        out_specs=(hbm, vmem),
        scratch_shapes=[pltpu.SemaphoreType.DMA, *Local.scratch(cells, late)],
        compiler_params=params,
        cost_estimate=pl.CostEstimate(flops=1 << 24, bytes_accessed=1 << 24, transcendentals=0),
        name="local_late",
    )(answers, table, rows, live, xyz, loc_early)
    loc_values, rem_values = pl.pallas_call(
        functools.partial(final_kernel, early),
        out_shape=(
            jax.ShapeDtypeStruct((5, loc), jnp.float32),
            jax.ShapeDtypeStruct((5, slots), jnp.float32),
        ),
        in_specs=[anyw, vmem, vmem, hbm],
        out_specs=(hbm, hbm),
        scratch_shapes=[pltpu.VMEM((5, slots), jnp.float32), pltpu.SemaphoreType.DMA((2,))],
        input_output_aliases={3: 0},
        compiler_params=params,
        name="final",
    )(live, stage, returned, loc_part)
    return (loc_values, rem_values)


def solution(mesh):
    placed = (
        P(None, "grid"),
        P(None, "grid"),
        P(None, ("grid", "help")),
        P(("grid", "help")),
        P("grid", "help"),
        P(None, ("grid", "help")),
        P(("grid", "help")),
        P(("grid", "help"), None),
    )
    return jax.shard_map(
        functools.partial(per_device, mesh.shape["help"]),
        mesh=mesh,
        in_specs=placed,
        out_specs=(P(None, ("grid", "help")), P(None, ("grid", "help"))),
        check_vma=False,
    )
```

```python
import functools
import jax
import jax.numpy as jnp
from jax import lax
from jax.experimental import pallas as pl
from jax.experimental.pallas import tpu as pltpu
from jax.sharding import PartitionSpec as P

PASSES = 3
LANES = 128
GROUP = 8 * LANES
ROWS = 64
VMEM_BYTES = 32 << 20
EARLY = 3
LEAD = 4
WIDEN = 32
QUARTERS = 4
STRIDE = 72


def monomials(corner):
    values = list(corner)
    for bit in (1, 2, 4):
        fresh = list(values)
        for k in range(8):
            if not k & bit:
                fresh[k] = values[k] + values[k | bit]
                fresh[k | bit] = values[k | bit] - values[k]
        values = fresh
    return values


def newton_step(jac, res):
    (a0, a1, a2), (b0, b1, b2), (c0, c1, c2) = jac
    k00 = b1 * c2 - b2 * c1
    k01 = b2 * c0 - b0 * c2
    k02 = b0 * c1 - b1 * c0
    k10 = a2 * c1 - a1 * c2
    k11 = a0 * c2 - a2 * c0
    k12 = a1 * c0 - a0 * c1
    k20 = a1 * b2 - a2 * b1
    k21 = a2 * b0 - a0 * b2
    k22 = a0 * b1 - a1 * b0
    inverse = 1.0 / (a0 * k00 + a1 * k01 + a2 * k02)
    return (
        (k00 * res[0] + k10 * res[1] + k20 * res[2]) * inverse,
        (k01 * res[0] + k11 * res[1] + k21 * res[2]) * inverse,
        (k02 * res[0] + k12 * res[1] + k22 * res[2]) * inverse,
    )


def newton(points, coef):
    step = newton_step(
        [[coef(i, 1), coef(i, 2), coef(i, 4)] for i in range(3)],
        [coef(i, 0) - points[i] for i in range(3)],
    )
    xi = [-s for s in step]
    for _ in range(PASSES - 1):
        x, y, z = xi
        jac, res = [], []
        for i in range(3):
            a0 = coef(i, 0) + coef(i, 4) * z
            a1 = coef(i, 1) + coef(i, 5) * z
            a2 = coef(i, 2) + coef(i, 6) * z
            a3 = coef(i, 3) + coef(i, 7) * z
            dx = a1 + a3 * y
            dy = a2 + a3 * x
            dz = (coef(i, 4) + coef(i, 6) * y) + (coef(i, 5) + coef(i, 7) * y) * x
            jac.append([dx, dy, dz])
            res.append((a0 + a2 * y) + dx * x - points[i])
        step = newton_step(jac, res)
        xi = [xi[d] - step[d] for d in range(3)]
    return xi


def blend(xi, value):
    low = [0.5 - 0.5 * v for v in xi]
    high = [0.5 + 0.5 * v for v in xi]
    plane = [p * q for q in (low[1], high[1]) for p in (low[0], high[0])]
    weights = [w * q for q in (low[2], high[2]) for w in plane]
    outs = []
    for f in range(5):
        total = weights[0] * value(24 + 8 * f)
        for k in range(1, 8):
            total = total + weights[k] * value(24 + 8 * f + k)
        outs.append(total)
    return outs


def wait_all(copies):
    for c in copies:
        c.start()
    for c in copies:
        c.wait()


def request_kernel(lead, xyz_hbm, cell_hbm, count_hbm, out_ref, xyz_ref, cell_ref, count_ref, sems):
    wait_all(
        [
            pltpu.make_async_copy(xyz_hbm, xyz_ref, sems.at[0]),
            pltpu.make_async_copy(cell_hbm, cell_ref, sems.at[1]),
            pltpu.make_async_copy(count_hbm, count_ref, sems.at[2]),
        ]
    )
    grid, depth, _ = out_ref.shape
    slots = xyz_ref.shape[1]
    width = -(-slots // LANES) * LANES
    wide = lambda a: a if a.shape[1] == width else jnp.pad(a, ((0, 0), (0, width - a.shape[1])))
    stack = jnp.concatenate(
        [
            jnp.zeros((ROWS, width), jnp.float32),
            wide(xyz_ref[...]),
            wide(cell_ref[...].astype(jnp.float32)),
            wide(count_ref[...].astype(jnp.float32)),
            jnp.zeros((LANES - ROWS - 5, width), jnp.float32),
        ],
        0,
    )
    turned = jnp.concatenate(
        [stack[:, k : k + LANES].T for k in range(0, width, LANES)], 0
    )
    counts = turned[0:grid, ROWS + 4 : ROWS + 5]
    lane = lax.broadcasted_iota(jnp.int32, (grid, LANES), 1)
    for c in range(depth):
        live = jnp.where(counts > float(c), 1.0, 0.0)
        whole = jnp.where(lane == ROWS + 4, live, turned[c * grid : (c + 1) * grid, :])
        out_ref[:, c, :] = jnp.concatenate([whole[lead:], whole[:lead]], 0) if lead else whole


class Local:
    @staticmethod
    def scratch(cells, groups):
        return [
            pltpu.VMEM((cells, LANES), jnp.float32),
            *[pltpu.SMEM((2, LANES), jnp.int32)] * QUARTERS,
            *[pltpu.VMEM((LANES, LANES), jnp.float32)] * QUARTERS,
            pltpu.VMEM(((groups + 1) * 8 * STRIDE, LANES), jnp.float32),
            pltpu.VMEM((24, 8, LANES), jnp.float32),
            pltpu.VMEM((3, 8, LANES), jnp.float32),
            pltpu.VMEM((64, LANES), jnp.float32),
            pltpu.VMEM((64, LANES), jnp.float32),
            pltpu.SemaphoreType.DMA((QUARTERS,)),
        ]

    def __init__(self, first, last, help_count, rows, live, xyz, stage, finished, *scratch):
        self.first, self.last, self.help_count = first, last, help_count
        self.rows, self.live, self.xyz, self.stage, self.finished = rows, live, xyz, stage, finished
        self.wide = scratch[0]
        self.smem, self.buf = scratch[1 : 1 + QUARTERS], scratch[1 + QUARTERS : 1 + 2 * QUARTERS]
        (self.turned, self.coefs, self.xi, self.points, self.outs, self.row_sems) = scratch[1 + 2 * QUARTERS :]

    def fetch(self, q, k):
        return pltpu.make_async_copy(self.rows.at[pl.ds(2 * (QUARTERS * self.first + q), 2), :], self.smem[k], self.row_sems.at[k])

    def turn(self, q, k):
        blocks = [self.buf[k + i][...].T for i in range(2)]
        for i in range(2):
            for h in range(2):
                at = pl.multiple_of((2 * (q + i) + 8 + h) * STRIDE, 8)
                self.turned[pl.ds(at, ROWS), :] = blocks[i][h * ROWS : (h + 1) * ROWS, :]

    def gather(self, k):
        for h in range(2):
            lanes = slice(h * ROWS, (h + 1) * ROWS)
            for j in range(LANES):
                self.buf[k][j : j + 1, lanes] = self.wide[pl.ds(self.smem[k][h, j], 1), lanes]

    def swap(self, table, lower=False):
        half = table.shape[0]

        def chunk(t, _):
            at = pl.multiple_of(t * LANES, LANES)
            both = table[pl.ds(at, LANES), :]
            if lower:
                self.wide[pl.ds(at, LANES), :] = both
            self.wide[pl.ds(pl.multiple_of(half + at, LANES), LANES), :] = pltpu.roll(both, ROWS, 1)
            return 0

        lax.fori_loop(0, half // LANES, chunk, 0, unroll=WIDEN)

    def begin(self):
        for k in range(QUARTERS):
            self.fetch(k, k).start()

    def run(self):
        groups = self.last - self.first
        stages = (lambda g: None, self.expand, self.solve, self.fields)

        def group(g, _):
            for k in range(QUARTERS):
                q = QUARTERS * g + k
                self.fetch(q, k).wait()
                self.gather(k)
                stages[k](g - 1)
                if k % 2 == 0:
                    self.turn(q - 2, (k - 2) % QUARTERS)

                @pl.when(g + 1 < groups)
                def _():
                    self.fetch(q + QUARTERS, k).start()

            @pl.when(g > 0)
            def _():
                self.finished(g - 1)

            return 0

        lax.fori_loop(0, groups, group, 0)
        self.turn(QUARTERS * groups - 2, QUARTERS - 2)
        for stage in stages:
            stage(groups - 1)
        self.finished(groups - 1)

    def value(self, g, v):
        return self.turned[pl.ds((g + 1) * 8 * STRIDE + v, 8, stride=STRIDE), :]

    def expand(self, g):
        for i in range(3):
            for k, c in enumerate(monomials([self.value(g, 8 * i + k) for k in range(8)])):
                self.coefs[8 * i + k] = c
        for b in range(8):
            at = pl.multiple_of(jnp.maximum(self.first + g, 0) * GROUP + b * LANES, LANES)
            self.points[b * 8 : b * 8 + 3, :] = self.xyz[:, pl.ds(at, LANES)]

    def solve(self, g):
        xi = newton(
            [self.points[pl.ds(d, 8, stride=8), :] for d in range(3)],
            lambda i, k: self.coefs[8 * i + k],
        )
        for d in range(3):
            self.xi[d] = xi[d]

    def fields(self, g):
        values = blend([self.xi[d] for d in range(3)], lambda v: self.value(g, v))
        slab = self.xyz.shape[1] // self.help_count
        slot = (
            (self.first + g) * GROUP
            + lax.broadcasted_iota(jnp.int32, (8, LANES), 0) * LANES
            + lax.broadcasted_iota(jnp.int32, (8, LANES), 1)
        )
        keep = lax.rem(slot, slab) * self.help_count + lax.div(slot, slab) < self.live[...]
        for f in range(5):
            self.outs[pl.ds(f, 8, stride=8), :] = jnp.where(keep, values[f], 0.0)
        for b in range(8):
            at = pl.multiple_of((g + 1) * GROUP + b * LANES, LANES)
            self.stage[:, pl.ds(at, LANES)] = self.outs[b * 8 : b * 8 + 5, :]


PIECES = 2


def first_kernel(last, help_count, _, corners_hbm, solution_hbm, cells_hbm, live_hbm, xyz_hbm, table, rows, live, xyz, stage, corners, solution, cells, live_one, sems, *scratch):
    local = Local(0, last, help_count, rows, live, xyz, stage, lambda g: None, *scratch)
    half = table.shape[0]
    piece = half // PIECES
    pieces = []
    for k in range(PIECES):
        for h in range(2):
            at = pl.ds(h * half + k * piece, piece)
            pieces.append(
                (
                    pltpu.make_async_copy(corners_hbm.at[:, at], corners.at[:, at], sems.at[4 * k + 2 * h]),
                    pltpu.make_async_copy(solution_hbm.at[:, at], solution.at[:, at], sems.at[4 * k + 2 * h + 1]),
                )
            )
    small = [
        pltpu.make_async_copy(cells_hbm, cells, sems.at[4 * PIECES]),
        pltpu.make_async_copy(xyz_hbm, xyz, sems.at[4 * PIECES + 1]),
        pltpu.make_async_copy(live_hbm, live_one, sems.at[4 * PIECES + 2]),
    ]
    for c in small[:1] + [c for pair in pieces for c in pair] + small[1:]:
        c.start()
    small[0].wait()
    whole = cells[...]
    other = jnp.where(whole >= half, whole - half, whole + half)
    odd = lax.rem(lax.broadcasted_iota(jnp.int32, whole.shape, 0), 2) == 1
    rows[...] = jnp.where(odd, other, whole)
    local.begin()
    for k in range(PIECES):
        for c in pieces[2 * k] + pieces[2 * k + 1]:
            c.wait()

        def chunk(t, _):
            low = pl.multiple_of(k * piece + t * LANES, LANES)
            high = pl.multiple_of(half + low, LANES)
            both = jnp.concatenate(
                [
                    corners[:, pl.ds(low, LANES)] * 0.125,
                    solution[:, pl.ds(low, LANES)],
                    corners[:, pl.ds(high, LANES)] * 0.125,
                    solution[:, pl.ds(high, LANES)],
                ],
                0,
            ).T
            table[pl.ds(low, LANES), :] = both
            local.wide[pl.ds(low, LANES), :] = both
            return 0

        lax.fori_loop(0, piece // LANES, chunk, 0, unroll=min(16, piece // LANES))
    local.swap(table)
    for c in small[1:]:
        c.wait()
    live[...] = jnp.broadcast_to(live_one[...], live.shape)
    local.run()


def second_kernel(first, last, help_count, _, table, rows, live, xyz, early, loc_hbm, stage, out_sem, *scratch):
    before = pltpu.make_async_copy(
        early.at[:, pl.ds(GROUP, first * GROUP)], loc_hbm.at[:, pl.ds(0, first * GROUP)], out_sem
    )
    before.start()
    local = Local(first, last, help_count, rows, live, xyz, stage, lambda g: None, *scratch)
    local.begin()
    local.swap(table, True)
    local.run()
    before.wait()


def final_kernel(first, _, stage, returned, before_hbm, loc_hbm, rem_hbm, total, sems):
    loc = pltpu.make_async_copy(
        stage.at[:, pl.ds(GROUP, stage.shape[1] - GROUP)],
        loc_hbm.at[:, pl.ds(first * GROUP, stage.shape[1] - GROUP)],
        sems.at[0],
    )
    loc.start()
    total[...] = jnp.sum(returned[...], axis=0)[0:5, 0 : total.shape[1]]
    rem = pltpu.make_async_copy(total, rem_hbm, sems.at[1])
    rem.start()
    loc.wait()
    rem.wait()


def answer_kernel(request_ref, table_ref, out_ref, rows, buf):
    grid, depth, _ = request_ref.shape
    half = table_ref.shape[0]
    blocks = out_ref.shape[2] // LANES
    mine = lax.axis_index("grid")
    for c in range(depth):
        rows[pl.ds(c * grid, grid), :] = request_ref[:, c, :]
    asked_all, cells = [], []
    for k in range(blocks):
        count = min(LANES, grid * depth - k * LANES)
        asked = rows[k * LANES : k * LANES + count, :]
        if count < LANES:
            asked = jnp.concatenate([asked, jnp.zeros((LANES - count, LANES), jnp.float32)], 0)
        asked_all.append(asked.T[ROWS : ROWS + 8, :])
        number = asked_all[k][3:4, :].astype(jnp.int32)
        cells.append(jnp.where(number >= half, number - half, number))
    lane = lax.broadcasted_iota(jnp.int32, (8, LANES), 1)
    for k in range(blocks):
        for j in range(min(LANES, grid * depth - k * LANES)):
            buf[j : j + 1, :] = table_ref[pl.ds(cells[k][0, j], 1), :]
        turned = buf[...].T
        asked = asked_all[k]
        upper = asked[3:4, :] >= float(half)
        value = lambda v: jnp.where(upper, turned[ROWS + v : ROWS + v + 1, :], turned[v : v + 1, :])
        coefs = [monomials([value(8 * i + k) for k in range(8)]) for i in range(3)]
        xi = newton([asked[d : d + 1, :] for d in range(3)], lambda i, k: coefs[i][k])
        results = blend(xi, value)
        keep = asked[4:5, :] > 0.5
        block = jnp.concatenate(
            [jnp.where(keep, r, 0.0) for r in results] + [jnp.zeros((3, LANES), jnp.float32)], 0
        )
        here = lax.rem(lane, grid) == mine

        def reply(r, _):
            moved = pltpu.roll(block, lax.rem(mine - r + LANES, LANES), 1)
            out_ref[r, :, k * LANES : (k + 1) * LANES] = jnp.where(here, moved, 0.0)
            return 0

        lax.fori_loop(0, grid, reply, 0, unroll=min(8, grid))


def per_device(help_count, corners, solution, loc_xyz, loc_cell, loc_live, rem_xyz, rem_cell, rem_count):
    grid = rem_count.shape[1]
    slots = rem_cell.shape[0]
    depth = slots // grid
    cells = corners.shape[1]
    loc = loc_cell.shape[0]
    early = EARLY
    lead = grid * LEAD // 8
    exchange = functools.partial(
        lax.all_to_all,
        axis_name="grid",
        split_axis=0,
        concat_axis=0,
        axis_index_groups=[[(j + lead) % grid for j in range(grid)]],
        tiled=True,
    )
    vmem = pl.BlockSpec(memory_space=pltpu.VMEM)
    hbm = pl.BlockSpec(memory_space=pltpu.HBM)
    anyw = pl.BlockSpec(memory_space=pl.ANY)
    params = pltpu.CompilerParams(vmem_limit_bytes=VMEM_BYTES)
    far = lambda a: pltpu.with_memory_space_constraint(a, pltpu.HBM)
    corners, solution, loc_xyz, rem_xyz, rem_count = map(far, (corners, solution, loc_xyz, rem_xyz, rem_count))
    cells2d = far(loc_cell.reshape(loc // LANES, LANES))
    rem_cell = far(rem_cell.reshape(1, slots))

    request = pl.pallas_call(
        functools.partial(request_kernel, lead),
        out_shape=jax.ShapeDtypeStruct((grid, depth, LANES), jnp.float32),
        in_specs=[hbm] * 3,
        out_specs=vmem,
        scratch_shapes=[
            pltpu.VMEM((3, slots), jnp.float32),
            pltpu.VMEM((1, slots), jnp.int32),
            pltpu.VMEM((1, grid), jnp.int32),
            pltpu.SemaphoreType.DMA((3,)),
        ],
        compiler_params=params,
        name="request",
    )(rem_xyz, rem_cell, rem_count)
    asked = exchange(request)
    table, rows, live, xyz, loc_early = pl.pallas_call(
        functools.partial(first_kernel, early, help_count),
        out_shape=(
            pltpu.VMEM((cells // 2, LANES), jnp.float32),
            pltpu.VMEM((loc // LANES, LANES), jnp.int32),
            pltpu.VMEM((8, LANES), jnp.int32),
            pltpu.VMEM((3, loc), jnp.float32),
            pltpu.VMEM((5, (early + 1) * GROUP), jnp.float32),
        ),
        in_specs=[anyw] + [hbm] * 5,
        out_specs=(vmem,) * 5,
        scratch_shapes=[
            pltpu.VMEM((24, cells), jnp.float32),
            pltpu.VMEM((40, cells), jnp.float32),
            pltpu.VMEM((loc // LANES, LANES), jnp.int32),
            pltpu.VMEM((1, 1), jnp.int32),
            pltpu.SemaphoreType.DMA((4 * PIECES + 3,)),
            *Local.scratch(cells, early),
        ],
        compiler_params=params,
        cost_estimate=pl.CostEstimate(flops=1 << 24, bytes_accessed=1 << 24, transcendentals=0),
        name="local_early",
    )(request, corners, solution, cells2d, loc_live, loc_xyz)
    width = -(-slots // LANES) * LANES
    answers = pl.pallas_call(
        answer_kernel,
        out_shape=jax.ShapeDtypeStruct((grid, 8, width), jnp.float32),
        in_specs=[vmem, vmem],
        out_specs=vmem,
        scratch_shapes=[
            pltpu.VMEM((slots, LANES), jnp.float32),
            pltpu.VMEM((LANES, LANES), jnp.float32),
        ],
        compiler_params=params,
        name="answer",
    )(asked, table)
    returned = exchange(answers)
    late = loc // GROUP - early
    loc_part, stage = pl.pallas_call(
        functools.partial(second_kernel, early, loc // GROUP, help_count),
        out_shape=(
            jax.ShapeDtypeStruct((5, loc), jnp.float32),
            pltpu.VMEM((5, (late + 1) * GROUP), jnp.float32),
        ),
        in_specs=[anyw] + [vmem] * 5,
        out_specs=(hbm, vmem),
        scratch_shapes=[pltpu.SemaphoreType.DMA, *Local.scratch(cells, late)],
        compiler_params=params,
        cost_estimate=pl.CostEstimate(flops=1 << 24, bytes_accessed=1 << 24, transcendentals=0),
        name="local_late",
    )(answers, table, rows, live, xyz, loc_early)
    loc_values, rem_values = pl.pallas_call(
        functools.partial(final_kernel, early),
        out_shape=(
            jax.ShapeDtypeStruct((5, loc), jnp.float32),
            jax.ShapeDtypeStruct((5, slots), jnp.float32),
        ),
        in_specs=[anyw, vmem, vmem, hbm],
        out_specs=(hbm, hbm),
        scratch_shapes=[pltpu.VMEM((5, slots), jnp.float32), pltpu.SemaphoreType.DMA((2,))],
        input_output_aliases={3: 0},
        compiler_params=params,
        name="final",
    )(live, stage, returned, loc_part)
    return (loc_values, rem_values)


def solution(mesh):
    placed = (
        P(None, "grid"),
        P(None, "grid"),
        P(None, ("grid", "help")),
        P(("grid", "help")),
        P("grid", "help"),
        P(None, ("grid", "help")),
        P(("grid", "help")),
        P(("grid", "help"), None),
    )
    return jax.shard_map(
        functools.partial(per_device, mesh.shape["help"]),
        mesh=mesh,
        in_specs=placed,
        out_specs=(P(None, ("grid", "help")), P(None, ("grid", "help"))),
        check_vma=False,
    )
```
